32 devices in a mesh: fsdp: 16 (over z, y, core), ctx: 2 (over x).
Axes of the slice: x: 2, y: 2, z: 4, core: 2. Of those that a mesh axis runs over, the one named last changes fastest.
Arguments:
- queries: bfloat16 [3328, 3072], P(('fsdp', 'ctx')), may hold values from -6 to 6
- keys: bfloat16 [3328, 3072], P(('fsdp', 'ctx')), may hold values from -6 to 6
- values: bfloat16 [3328, 3072], P(('fsdp', 'ctx')), may hold values from -6 to 6
- norm_gain: float32 [3072], replicated, may hold values from 0.1 to 1.9
- out_weight: bfloat16 [3072, 3072], P('fsdp', 'ctx'), may hold values from -0.109375 to 0.109375
Outputs:
- layer_out: bfloat16 [3328, 3072], P('fsdp', 'ctx')
The draws below stay inside these ranges and needn't reach their ends.
All inputs are finite; a program needn't handle non-finite values.
Results may differ from the reference program's by a relative error of at most 0.0061.
Values may be sent and summed in bfloat16 or wider, within the bound.
A program may use at most 64 MiB of HBM per device.

```python
import jax
import jax.numpy as jnp
from jax import lax

HEADS = 32
HEAD_DIM = 96
D = 3072
TOK_DEV = 104
HD = 3072
SEQ_LEN = 208
TOKENS = 3328
N_CTX = 2


def steps_of(key, extent, pieces, least, largest):
    factor_of, own = 1.0, jax.random.fold_in(key, 6)
    for dim, blocks in pieces:
        steps = jnp.exp(jax.random.uniform(jax.random.fold_in(own, dim), (blocks,), jnp.float32, least / len(pieces), largest / len(pieces)))
        factor_of = factor_of * jnp.repeat(steps, extent[dim] // blocks).reshape([-1 if axis == dim else 1 for axis in range(len(extent))])
    return factor_of


def gaussian(stream_key, dims, scale, reach, shards=(), dtype=jnp.bfloat16):
    factor_of = steps_of(stream_key, dims, shards, -0.22, 0.18) if shards else 1.0
    values = jax.random.normal(stream_key, dims, jnp.float32) * scale * factor_of
    return jnp.minimum(jnp.maximum(values, -reach), reach).astype(dtype)


def setup_inputs(seed: int = 0) -> dict:
    streams_of = jax.random.split(jax.random.key(seed), 6)
    return {
        "queries": gaussian(streams_of[0], (TOKENS, HD), 1.0, 6.0, ((0, 32),)),
        "keys": gaussian(streams_of[1], (TOKENS, HD), 1.0, 6.0, ((0, 32),)),
        "values": gaussian(streams_of[2], (TOKENS, HD), 1.0, 6.0, ((0, 32),)),
        "norm_gain": jnp.clip(1.0 + 0.18 * jax.random.normal(streams_of[3], (HD,), jnp.float32), 0.1, 1.9),
        "out_weight": gaussian(streams_of[4], (HD, D), HD ** -0.5, 0.109375, ((0, 16), (1, 2))),
    }


def one_sequence(items, norm_gain):
    q_blocks, k_blocks, v_blocks = items
    causal = jnp.arange(TOK_DEV)[:, None] >= jnp.arange(TOK_DEV)[None, :]

    def step(running, parts):
        q_block = parts[0].astype(jnp.float32)
        k_block = parts[1].astype(jnp.float32)
        v_block = parts[2].astype(jnp.float32)
        scores = jnp.einsum('thd,shd->hts', q_block, k_block)
        scores = jnp.where(causal, scores, 0.0).astype(jnp.bfloat16)
        intra = jnp.einsum('hts,shd->thd', scores.astype(jnp.float32), v_block)
        local_state = jnp.einsum('shd,she->hde', k_block, v_block).astype(jnp.bfloat16)
        prefix_state = running.astype(jnp.bfloat16)
        inter = jnp.einsum('thd,hde->the', q_block, prefix_state.astype(jnp.float32))
        attn = (intra + inter).reshape(TOK_DEV, HD)
        mean_sq = lax.optimization_barrier(jnp.mean(attn * attn, axis=-1, keepdims=True))
        normed = (attn * lax.rsqrt(mean_sq + 1e-05) * norm_gain).astype(jnp.bfloat16)
        return (running + local_state.astype(jnp.float32), normed)
    start = jnp.zeros((HEADS, HEAD_DIM, HEAD_DIM), jnp.float32)
    final_state, normed_seq = lax.scan(step, start, (q_blocks, k_blocks, v_blocks))
    return normed_seq

def reference(queries, keys, values, norm_gain, out_weight):
    sequences = TOKENS // SEQ_LEN
    shape = (sequences, N_CTX, TOK_DEV, HEADS, HEAD_DIM)
    normed_all = lax.map(lambda items: one_sequence(items, norm_gain), (queries.reshape(shape), keys.reshape(shape), values.reshape(shape)))
    normed_all = normed_all.reshape(TOKENS, HD)
    return jnp.dot(normed_all, out_weight, preferred_element_type=jnp.float32).astype(jnp.bfloat16)
```

```python
import functools

import jax
import jax.numpy as jnp
from jax import lax
from jax.experimental import pallas as pl
from jax.experimental.pallas import tpu as pltpu
from jax.sharding import PartitionSpec as P

HEADS = 32
HEAD_DIM = 96
MESH = pl.DeviceIdType.MESH
BF16 = jnp.bfloat16
F32 = jnp.float32


def on_device(queries, keys, values, norm_gain, out_weight):
    tok_rows = queries.shape[0]
    q_heads = queries.reshape(tok_rows, HEADS, HEAD_DIM)
    k_heads = keys.reshape(tok_rows, HEADS, HEAD_DIM)
    v_heads = values.reshape(tok_rows, HEADS, HEAD_DIM)
    scores = jnp.einsum("thd,shd->hts", q_heads, k_heads, preferred_element_type=jnp.float32)
    causal = jnp.arange(tok_rows)[:, None] >= jnp.arange(tok_rows)[None, :]
    scores = jnp.where(causal, scores, 0.0).astype(jnp.bfloat16)
    intra = jnp.einsum("hts,shd->thd", scores, v_heads, preferred_element_type=jnp.float32)
    local_state = jnp.einsum("shd,she->hde", k_heads, v_heads, preferred_element_type=jnp.float32)
    flat_state = local_state.reshape(HEADS, HEAD_DIM * HEAD_DIM).astype(jnp.bfloat16)
    every_state = lax.all_gather(flat_state[None], "ctx", axis=0, tiled=True)
    position = lax.axis_index("ctx")
    earlier = (jnp.arange(every_state.shape[0]) < position)[:, None, None]
    prefix_flat = jnp.sum(jnp.where(earlier, every_state.astype(jnp.float32), 0.0), axis=0)
    prefix_state = prefix_flat.reshape(HEADS, HEAD_DIM, HEAD_DIM).astype(jnp.bfloat16)
    inter = jnp.einsum("thd,hde->the", q_heads, prefix_state, preferred_element_type=jnp.float32)
    attn = (intra + inter).reshape(tok_rows, HEADS * HEAD_DIM)
    mean_sq = jnp.mean(attn * attn, axis=-1, keepdims=True)
    normed = (attn * lax.rsqrt(mean_sq + 1e-05) * norm_gain).astype(jnp.bfloat16)
    weight_block = lax.all_gather(out_weight, "fsdp", axis=0, tiled=True)
    result = jnp.dot(
        lax.all_gather(normed, "ctx", axis=0, tiled=True),
        weight_block,
        preferred_element_type=jnp.float32,
    )
    return result.astype(jnp.bfloat16)


def kernel(
    planes, q_ref, k_ref, v_ref, gain_ref, w_ref, out_ref,
    w_all, state_own, state_in, x_out, x_all, x_cat, att, ms, acc, part_out, part_in,
    w_load, w_send, w_recv, state_send, state_recv, x_send, x_recv, ms_send, ms_recv,
    part_send, part_recv,
):
    tok, features = q_ref.shape
    rows = w_ref.shape[0]
    width = 2 * rows
    chunk = w_ref.shape[1] // planes
    group_heads = width // HEAD_DIM

    f = lax.axis_index("fsdp")
    x = lax.axis_index("ctx")
    z, y, c = lax.div(f, 4), lax.rem(lax.div(f, 2), 2), lax.rem(f, 2)

    def at(zz, yy, cc, xx):
        return (4 * zz + 2 * yy + cc, xx)

    sibling = at(z, y, 1 - c, x)
    across = at(z, y, c, 1 - x)
    beside = at(z, 1 - y, c, x)
    diagonal = at(z, 1 - y, c, 1 - x)

    def remote(src, dst, send, recv, device):
        return pltpu.make_async_remote_copy(
            src_ref=src, dst_ref=dst, send_sem=send, recv_sem=recv,
            device_id=device, device_id_type=MESH,
        )

    def load(j):
        return pltpu.make_async_copy(
            w_ref.at[:, pl.ds(pl.multiple_of(j * chunk, chunk), chunk)],
            w_all.at[j, z, c], w_load.at[j],
        )

    def w_copy(j, plane, way):
        device = (at(z - 1, y, c, x), at(z + 1, y, c, x), sibling)[way]
        block = w_all.at[j, plane, c]
        return remote(block, block, w_send.at[j, plane, way], w_recv.at[j, plane, c], device)

    def w_arrive(j, plane, core):
        block = w_all.at[j, plane, core]
        remote(block, block, w_send.at[j, plane, 2], w_recv.at[j, plane, core], sibling).wait_recv()

    def each(body):
        def step(i, carry):
            body(i)
            return carry
        lax.fori_loop(0, planes, step, 0)

    each(lambda j: load(j).start())

    barrier = pltpu.get_barrier_semaphore()
    for device in (sibling, across, beside, diagonal):
        pl.semaphore_signal(barrier, inc=1, device_id=device, device_id_type=MESH)

    @pl.when(z > 0)
    def _():
        pl.semaphore_signal(barrier, inc=1, device_id=at(z - 1, y, c, x), device_id_type=MESH)

    @pl.when(z < planes - 1)
    def _():
        pl.semaphore_signal(barrier, inc=1, device_id=at(z + 1, y, c, x), device_id_type=MESH)

    pl.semaphore_wait(barrier, 4 + jnp.where(z > 0, 1, 0) + jnp.where(z < planes - 1, 1, 0))

    def send_own(j):
        load(j).wait()

        @pl.when(z > 0)
        def _():
            w_copy(j, z, 0).start()

        @pl.when(z < planes - 1)
        def _():
            w_copy(j, z, 1).start()

        w_copy(j, z, 2).start()

    each(send_own)

    lane = lax.broadcasted_iota(jnp.int32, (1, width), 1)
    in_head = [
        jnp.where((lane >= h * HEAD_DIM) & (lane < (h + 1) * HEAD_DIM), 1.0, 0.0)
        for h in range(group_heads)
    ]
    in_head16 = [m.astype(BF16) for m in in_head]

    def columns(i, yy):
        return pl.ds(pl.multiple_of(i * (2 * width), 2 * width) + yy * width, width)

    def state_copy(i, yy):
        return remote(
            state_own.at[i, yy], state_in.at[i, yy], state_send.at[i, yy], state_recv.at[i, yy], across
        )

    @pl.when(x == 0)
    def _():
        def states(i):
            for yy in range(2):
                full = lax.dot_general(
                    k_ref[:, columns(i, yy)], v_ref[:, columns(i, yy)],
                    (((0,), (0,)), ((), ())), preferred_element_type=F32,
                )
                folded = full[:HEAD_DIM] * in_head[0]
                for h in range(1, group_heads):
                    folded = folded + full[h * HEAD_DIM:(h + 1) * HEAD_DIM] * in_head[h]
                state_own[i, yy] = folded.astype(BF16)
                state_copy(i, yy).start()
        each(states)

    def pass_on(j, distance):
        @pl.when(z - distance >= 0)
        def _():
            w_arrive(j, z - distance, c)

            @pl.when(z < planes - 1)
            def _():
                w_copy(j, z - distance, 1).start()

            w_copy(j, z - distance, 2).start()

        @pl.when(z + distance < planes)
        def _():
            w_arrive(j, z + distance, c)

            @pl.when(z > 0)
            def _():
                w_copy(j, z + distance, 0).start()

            w_copy(j, z + distance, 2).start()

    def x_near(i, yy):
        return remote(
            x_out.at[i, yy], x_all.at[i, y, x], x_send.at[i, yy, 0], x_recv.at[i, y, x], at(z, yy, c, x)
        )

    def x_far(i, yy):
        return remote(
            x_out.at[i, yy], x_all.at[i, y, x], x_send.at[i, yy, 1], x_recv.at[i, y, x],
            at(z, yy, c, 1 - x),
        )

    causal = (
        lax.broadcasted_iota(jnp.int32, (tok, tok), 0) >= lax.broadcasted_iota(jnp.int32, (tok, tok), 1)
    )
    ms[x] = jnp.zeros(ms.shape[1:], F32)

    def attend(i):
        for yy in range(2):
            q, k, v = (ref[:, columns(i, yy)] for ref in (q_ref, k_ref, v_ref))
            total = jnp.zeros((tok, width), F32)
            for h in range(group_heads):
                scores = lax.dot_general(
                    q * in_head16[h], k, (((1,), (1,)), ((), ())), preferred_element_type=F32
                )
                scores = jnp.where(causal, scores, 0.0).astype(BF16)
                total = total + jnp.dot(scores, v * in_head16[h], preferred_element_type=F32)
            att[...] = total

            @pl.when(x == 1)
            def _():
                state_copy(i, yy).wait_recv()
                state = state_in[i, yy]
                wide = jnp.concatenate([state * m for m in in_head16], axis=0)
                att[...] += jnp.dot(q, wide, preferred_element_type=F32)

            attn = att[...]
            ms[x] += jnp.broadcast_to(
                jnp.sum(attn * attn, axis=-1, keepdims=True) * (1.0 / features), ms.shape[1:]
            )
            scaled = (attn * gain_ref[:, columns(i, yy)]).astype(BF16)
            x_out[i, yy] = scaled
            x_far(i, yy).start()

            @pl.when(y != yy)
            def _():
                x_near(i, yy).start()

            @pl.when(y == yy)
            def _():
                x_all[i, y, x] = scaled

        pass_on(i, 1)

    each(attend)
    ms_copy = remote(ms.at[x], ms.at[x], ms_send, ms_recv, across)
    ms_copy.start()

    for distance in range(2, planes - 1):
        each(functools.partial(pass_on, distance=distance))

    def x_arrive(i, yy, xx):
        remote(
            x_all.at[i, yy, xx], x_all.at[i, yy, xx], x_send.at[i, yy, 1], x_recv.at[i, yy, xx], across
        ).wait_recv()

    def merge(i):
        x_arrive(i, y, 1 - x)
        x_arrive(i, 1 - y, x)
        x_arrive(i, 1 - y, 1 - x)
        parts = [x_all[i, yy, xx].astype(F32) for yy in range(2) for xx in range(2)]
        x_cat[i] = jnp.concatenate(parts, axis=0).astype(BF16)

    each(merge)

    def multiply(j, plane):
        w_arrive(j, plane, 1 - c)
        return jnp.dot(
            x_cat[plane], w_all[j, plane].reshape(width, chunk), preferred_element_type=F32
        )

    def first(j):
        total = multiply(j, z)
        acc[j, 0] = total[:2 * tok]
        acc[j, 1] = total[2 * tok:]

    each(first)

    def add(j, plane):
        total = multiply(j, plane)
        acc[j, 0] += total[:2 * tok]
        acc[j, 1] += total[2 * tok:]

    def add_both(j, distance):
        @pl.when(z - distance >= 0)
        def _():
            add(j, z - distance)

        @pl.when(z + distance < planes)
        def _():
            add(j, z + distance)

    for distance in range(1, planes - 1):
        each(functools.partial(add_both, distance=distance))

    def part_copy(j):
        return remote(part_out.at[j], part_in.at[j], part_send.at[j], part_recv.at[j], beside)

    def last(j):
        pass_on(j, planes - 1)
        add_both(j, planes - 1)
        part_out[j] = acc[j, 1 - y].astype(BF16)
        part_copy(j).start()

    each(last)

    remote(ms.at[1 - x], ms.at[1 - x], ms_send, ms_recv, across).wait_recv()
    mean_sq = jnp.concatenate([ms[0][:, :1], ms[1][:, :1]], axis=0)
    scale = lax.rsqrt(mean_sq + 1e-05)

    def finish(j):
        part_copy(j).wait_recv()
        total = acc[j, y] + part_in[j].astype(F32)
        out_ref[:, pl.ds(pl.multiple_of(j * chunk, chunk), chunk)] = (total * scale).astype(BF16)

    each(finish)

    def drain(i):
        part_copy(i).wait_send()
        for yy in range(2):
            x_far(i, yy).wait_send()

            @pl.when(y != yy)
            def _():
                x_near(i, yy).wait_send()

            @pl.when(x == 0)
            def _():
                state_copy(i, yy).wait_send()

        for plane in range(planes):
            w_copy(i, plane, 2).wait_send()

            @pl.when((plane >= z) & (z > 0))
            def _():
                w_copy(i, plane, 0).wait_send()

            @pl.when((plane <= z) & (z < planes - 1))
            def _():
                w_copy(i, plane, 1).wait_send()

    each(drain)
    ms_copy.wait_send()


def fused(planes, queries, keys, values, norm_gain, out_weight):
    tok, features = queries.shape
    rows, out_columns = out_weight.shape
    width, chunk = 2 * rows, out_columns // planes
    vmem = pl.BlockSpec(memory_space=pltpu.VMEM)
    dma = pltpu.SemaphoreType.DMA
    return pl.pallas_call(
        functools.partial(kernel, planes),
        out_shape=jax.ShapeDtypeStruct((2 * tok, out_columns), BF16),
        in_specs=[vmem, vmem, vmem, vmem, pl.BlockSpec(memory_space=pl.ANY)],
        out_specs=vmem,
        scratch_shapes=[
            pltpu.VMEM((planes, planes, 2, rows, chunk), BF16),
            pltpu.VMEM((planes, 2, HEAD_DIM, width), BF16),
            pltpu.VMEM((planes, 2, HEAD_DIM, width), BF16),
            pltpu.VMEM((planes, 2, tok, width), BF16),
            pltpu.VMEM((planes, 2, 2, tok, width), BF16),
            pltpu.VMEM((planes, 4 * tok, width), BF16),
            pltpu.VMEM((tok, width), F32),
            pltpu.VMEM((2, tok, 128), F32),
            pltpu.VMEM((planes, 2, 2 * tok, chunk), F32),
            pltpu.VMEM((planes, 2 * tok, chunk), BF16),
            pltpu.VMEM((planes, 2 * tok, chunk), BF16),
            dma((planes,)),
            dma((planes, planes, 3)),
            dma((planes, planes, 2)),
            dma((planes, 2)),
            dma((planes, 2)),
            dma((planes, 2, 2)),
            dma((planes, 2, 2)),
            dma,
            dma,
            dma((planes,)),
            dma((planes,)),
        ],
        compiler_params=pltpu.CompilerParams(
            collective_id=0, has_side_effects=True, vmem_limit_bytes=40 * 1024 * 1024
        ),
    )(queries, keys, values, norm_gain.reshape(1, features), out_weight)


def solution(mesh):
    placed = (
        P(("fsdp", "ctx"), None),
        P(("fsdp", "ctx"), None),
        P(("fsdp", "ctx"), None),
        P(),
        P("fsdp", "ctx"),
    )
    planes = mesh.shape["fsdp"] // 4

    def body(queries, keys, values, norm_gain, out_weight):
        rows, out_columns = out_weight.shape
        width = 2 * rows
        fits = (
            mesh.shape["ctx"] == 2
            and mesh.shape["fsdp"] == 4 * planes
            and 3 <= planes <= 4
            and rows % 16 == 0
            and width % HEAD_DIM == 0
            and width % 128 == 0
            and out_columns % (128 * planes) == 0
        )
        if fits:
            return fused(planes, queries, keys, values, norm_gain, out_weight)
        return on_device(queries, keys, values, norm_gain, out_weight)

    return jax.shard_map(
        body, mesh=mesh, in_specs=placed, out_specs=P("fsdp", "ctx"), check_vma=False
    )
```

```python
import functools

import jax
import jax.numpy as jnp
from jax import lax
from jax.experimental import pallas as pl
from jax.experimental.pallas import tpu as pltpu
from jax.sharding import PartitionSpec as P

HEADS = 32
HEAD_DIM = 96
MESH = pl.DeviceIdType.MESH
BF16 = jnp.bfloat16
F32 = jnp.float32


def on_device(queries, keys, values, norm_gain, out_weight):
    tok_rows = queries.shape[0]
    q_heads = queries.reshape(tok_rows, HEADS, HEAD_DIM)
    k_heads = keys.reshape(tok_rows, HEADS, HEAD_DIM)
    v_heads = values.reshape(tok_rows, HEADS, HEAD_DIM)
    scores = jnp.einsum("thd,shd->hts", q_heads, k_heads, preferred_element_type=jnp.float32)
    causal = jnp.arange(tok_rows)[:, None] >= jnp.arange(tok_rows)[None, :]
    scores = jnp.where(causal, scores, 0.0).astype(jnp.bfloat16)
    intra = jnp.einsum("hts,shd->thd", scores, v_heads, preferred_element_type=jnp.float32)
    local_state = jnp.einsum("shd,she->hde", k_heads, v_heads, preferred_element_type=jnp.float32)
    flat_state = local_state.reshape(HEADS, HEAD_DIM * HEAD_DIM).astype(jnp.bfloat16)
    every_state = lax.all_gather(flat_state[None], "ctx", axis=0, tiled=True)
    position = lax.axis_index("ctx")
    earlier = (jnp.arange(every_state.shape[0]) < position)[:, None, None]
    prefix_flat = jnp.sum(jnp.where(earlier, every_state.astype(jnp.float32), 0.0), axis=0)
    prefix_state = prefix_flat.reshape(HEADS, HEAD_DIM, HEAD_DIM).astype(jnp.bfloat16)
    inter = jnp.einsum("thd,hde->the", q_heads, prefix_state, preferred_element_type=jnp.float32)
    attn = (intra + inter).reshape(tok_rows, HEADS * HEAD_DIM)
    mean_sq = jnp.mean(attn * attn, axis=-1, keepdims=True)
    normed = (attn * lax.rsqrt(mean_sq + 1e-05) * norm_gain).astype(jnp.bfloat16)
    weight_block = lax.all_gather(out_weight, "fsdp", axis=0, tiled=True)
    result = jnp.dot(
        lax.all_gather(normed, "ctx", axis=0, tiled=True),
        weight_block,
        preferred_element_type=jnp.float32,
    )
    return result.astype(jnp.bfloat16)


def kernel(
    planes, chunks, q_in, k_in, v_in, gain_in, w_ref, out_ref,
    q_ref, k_ref, v_ref, gain_ref, w_all, out_all, state_own, state_in, x_out, x_all, x_cat, att, ms, acc, part_out, part_in,
    w_load, w_send, w_recv, state_send, state_recv, x_send, x_recv, ms_send, ms_recv,
    part_send, part_recv, in_load, out_store,
):
    tok, features = q_ref.shape
    rows = w_ref.shape[0]
    width = 2 * rows
    chunk = w_ref.shape[1] // chunks
    group_heads = width // HEAD_DIM

    f = lax.axis_index("fsdp")
    x = lax.axis_index("ctx")
    z, y, c = lax.div(f, 4), lax.rem(lax.div(f, 2), 2), lax.rem(f, 2)

    def at(zz, yy, cc, xx):
        return (4 * zz + 2 * yy + cc, xx)

    sibling = at(z, y, 1 - c, x)
    across = at(z, y, c, 1 - x)
    beside = at(z, 1 - y, c, x)
    diagonal = at(z, 1 - y, c, 1 - x)

    def remote(src, dst, send, recv, device):
        return pltpu.make_async_remote_copy(
            src_ref=src, dst_ref=dst, send_sem=send, recv_sem=recv,
            device_id=device, device_id_type=MESH,
        )

    def load(j):
        return pltpu.make_async_copy(
            w_ref.at[:, pl.ds(pl.multiple_of(j * chunk, chunk), chunk)],
            w_all.at[j, z, c], w_load.at[j],
        )

    def w_copy(j, plane, way):
        device = (at(z - 1, y, c, x), at(z + 1, y, c, x), sibling)[way]
        block = w_all.at[j, plane, c]
        return remote(block, block, w_send.at[j, plane, way], w_recv.at[j, plane, c], device)

    def w_arrive(j, plane, core):
        block = w_all.at[j, plane, core]
        remote(block, block, w_send.at[j, plane, 2], w_recv.at[j, plane, core], sibling).wait_recv()

    def each(body, count=planes):
        def step(i, carry):
            body(i)
            return carry
        lax.fori_loop(0, count, step, 0)

    every_chunk = functools.partial(each, count=chunks)
    every_chunk(lambda j: load(j).start())
    inputs = [
        pltpu.make_async_copy(src, dst, in_load.at[n])
        for n, (src, dst) in enumerate(
            ((k_in, k_ref), (v_in, v_ref), (q_in, q_ref), (gain_in, gain_ref))
        )
    ]
    for copy in inputs:
        copy.start()

    barrier = pltpu.get_barrier_semaphore()
    for device in (sibling, across, beside, diagonal):
        pl.semaphore_signal(barrier, inc=1, device_id=device, device_id_type=MESH)

    @pl.when(z > 0)
    def _():
        pl.semaphore_signal(barrier, inc=1, device_id=at(z - 1, y, c, x), device_id_type=MESH)

    @pl.when(z < planes - 1)
    def _():
        pl.semaphore_signal(barrier, inc=1, device_id=at(z + 1, y, c, x), device_id_type=MESH)

    pl.semaphore_wait(barrier, 4 + jnp.where(z > 0, 1, 0) + jnp.where(z < planes - 1, 1, 0))

    def send_own(j):
        load(j).wait()

        @pl.when(z > 0)
        def _():
            w_copy(j, z, 0).start()

        @pl.when(z < planes - 1)
        def _():
            w_copy(j, z, 1).start()

        w_copy(j, z, 2).start()

    every_chunk(send_own)
    for copy in inputs:
        copy.wait()

    lane = lax.broadcasted_iota(jnp.int32, (1, width), 1)
    in_head = [
        jnp.where((lane >= h * HEAD_DIM) & (lane < (h + 1) * HEAD_DIM), 1.0, 0.0)
        for h in range(group_heads)
    ]
    in_head16 = [m.astype(BF16) for m in in_head]

    def columns(i, yy):
        return pl.ds(pl.multiple_of(i * (2 * width), 2 * width) + yy * width, width)

    def state_copy(i, yy):
        return remote(
            state_own.at[i, yy], state_in.at[i, yy], state_send.at[i, yy], state_recv.at[i, yy], across
        )

    @pl.when(x == 0)
    def _():
        def states(i):
            for yy in range(2):
                full = lax.dot_general(
                    k_ref[:, columns(i, yy)], v_ref[:, columns(i, yy)],
                    (((0,), (0,)), ((), ())), preferred_element_type=F32,
                )
                folded = full[:HEAD_DIM] * in_head[0]
                for h in range(1, group_heads):
                    folded = folded + full[h * HEAD_DIM:(h + 1) * HEAD_DIM] * in_head[h]
                state_own[i, yy] = folded.astype(BF16)
                state_copy(i, yy).start()
        each(states)

    def pass_on(j, distance):
        @pl.when(z - distance >= 0)
        def _():
            w_arrive(j, z - distance, c)

            @pl.when(z < planes - 1)
            def _():
                w_copy(j, z - distance, 1).start()

            w_copy(j, z - distance, 2).start()

        @pl.when(z + distance < planes)
        def _():
            w_arrive(j, z + distance, c)

            @pl.when(z > 0)
            def _():
                w_copy(j, z + distance, 0).start()

            w_copy(j, z + distance, 2).start()

    def x_near(i, yy):
        return remote(
            x_out.at[i, yy], x_all.at[i, y, x], x_send.at[i, yy, 0], x_recv.at[i, y, x], at(z, yy, c, x)
        )

    def x_far(i, yy):
        return remote(
            x_out.at[i, yy], x_all.at[i, y, x], x_send.at[i, yy, 1], x_recv.at[i, y, x],
            at(z, yy, c, 1 - x),
        )

    causal = (
        lax.broadcasted_iota(jnp.int32, (tok, tok), 0) >= lax.broadcasted_iota(jnp.int32, (tok, tok), 1)
    )
    ms[x] = jnp.zeros(ms.shape[1:], F32)

    def pass_on_share(i, distance):
        share = chunks // planes
        each(lambda n: pass_on(i * share + n, distance), share)

    def deliver(i, yy, attn):
        ms[x] += jnp.broadcast_to(
            jnp.sum(attn * attn, axis=-1, keepdims=True) * (1.0 / features), ms.shape[1:]
        )
        scaled = (attn * gain_ref[:, columns(i, yy)]).astype(BF16)
        x_out[i, yy] = scaled
        x_far(i, yy).start()

        @pl.when(y != yy)
        def _():
            x_near(i, yy).start()

        @pl.when(y == yy)
        def _():
            x_all[i, y, x] = scaled

    def attend(i):
        for yy in range(2):
            q, k, v = (ref[:, columns(i, yy)] for ref in (q_ref, k_ref, v_ref))
            total = jnp.zeros((tok, width), F32)
            for h in range(group_heads):
                scores = lax.dot_general(
                    q * in_head16[h], k, (((1,), (1,)), ((), ())), preferred_element_type=F32
                )
                scores = jnp.where(causal, scores, 0.0).astype(BF16)
                total = total + jnp.dot(scores, v * in_head16[h], preferred_element_type=F32)
            att[i, yy] = total

            @pl.when(x == 0)
            def _():
                deliver(i, yy, att[i, yy])

        pass_on_share(i, 1)

    each(attend)

    def attend_earlier(i):
        @pl.when(x == 1)
        def _():
            for yy in range(2):
                state_copy(i, yy).wait_recv()
                state = state_in[i, yy]
                wide = jnp.concatenate([state * m for m in in_head16], axis=0)
                inter = jnp.dot(q_ref[:, columns(i, yy)], wide, preferred_element_type=F32)
                deliver(i, yy, att[i, yy] + inter)

        pass_on_share(i, 2)

    each(attend_earlier)
    ms_copy = remote(ms.at[x], ms.at[x], ms_send, ms_recv, across)
    ms_copy.start()

    def x_arrive(i, yy, xx):
        remote(
            x_all.at[i, yy, xx], x_all.at[i, yy, xx], x_send.at[i, yy, 1], x_recv.at[i, yy, xx], across
        ).wait_recv()

    def merge(i):
        x_arrive(i, y, 1 - x)
        x_arrive(i, 1 - y, x)
        x_arrive(i, 1 - y, 1 - x)
        parts = [x_all[i, yy, xx].astype(F32) for yy in range(2) for xx in range(2)]
        x_cat[i] = jnp.concatenate(parts, axis=0).astype(BF16)

    each(merge)

    def multiply(j, plane):
        w_arrive(j, plane, 1 - c)
        return jnp.dot(
            x_cat[plane], w_all[j, plane].reshape(width, chunk), preferred_element_type=F32
        )

    def first(j):
        total = multiply(j, z)
        acc[j, 0] = total[:2 * tok]
        acc[j, 1] = total[2 * tok:]

    every_chunk(first)

    def add(j, plane):
        total = multiply(j, plane)
        acc[j, 0] += total[:2 * tok]
        acc[j, 1] += total[2 * tok:]

    def add_both(j, distance):
        @pl.when(z - distance >= 0)
        def _():
            add(j, z - distance)

        @pl.when(z + distance < planes)
        def _():
            add(j, z + distance)

    for distance in range(1, planes - 1):
        every_chunk(functools.partial(add_both, distance=distance))

    def part_copy(j):
        return remote(part_out.at[j], part_in.at[j], part_send.at[j], part_recv.at[j], beside)

    def last(j):
        pass_on(j, planes - 1)
        add_both(j, planes - 1)
        part_out[j] = acc[j, 1 - y].astype(BF16)
        part_copy(j).start()

    every_chunk(last)

    remote(ms.at[1 - x], ms.at[1 - x], ms_send, ms_recv, across).wait_recv()
    mean_sq = jnp.concatenate([ms[0][:, :1], ms[1][:, :1]], axis=0)
    scale = lax.rsqrt(mean_sq + 1e-05)

    def store(j):
        return pltpu.make_async_copy(
            out_all.at[j],
            out_ref.at[:, pl.ds(pl.multiple_of(j * chunk, chunk), chunk)], out_store.at[j],
        )

    def finish(j):
        part_copy(j).wait_recv()
        total = acc[j, y] + part_in[j].astype(F32)
        out_all[j] = (total * scale).astype(BF16)
        store(j).start()

    every_chunk(finish)

    def drain(i):
        for yy in range(2):
            x_far(i, yy).wait_send()

            @pl.when(y != yy)
            def _():
                x_near(i, yy).wait_send()

            @pl.when(x == 0)
            def _():
                state_copy(i, yy).wait_send()

    def drain_chunk(i):
        part_copy(i).wait_send()
        store(i).wait()

        for plane in range(planes):
            w_copy(i, plane, 2).wait_send()

            @pl.when((plane >= z) & (z > 0))
            def _():
                w_copy(i, plane, 0).wait_send()

            @pl.when((plane <= z) & (z < planes - 1))
            def _():
                w_copy(i, plane, 1).wait_send()

    each(drain)
    every_chunk(drain_chunk)
    ms_copy.wait_send()


def fused(planes, chunks, queries, keys, values, norm_gain, out_weight):
    tok, features = queries.shape
    rows, out_columns = out_weight.shape
    width, chunk = 2 * rows, out_columns // chunks
    anywhere = pl.BlockSpec(memory_space=pl.ANY)
    dma = pltpu.SemaphoreType.DMA
    return pl.pallas_call(
        functools.partial(kernel, planes, chunks),
        out_shape=jax.ShapeDtypeStruct((2 * tok, out_columns), BF16),
        in_specs=[anywhere] * 5,
        out_specs=anywhere,
        scratch_shapes=[
            pltpu.VMEM((tok, features), BF16),
            pltpu.VMEM((tok, features), BF16),
            pltpu.VMEM((tok, features), BF16),
            pltpu.VMEM((1, features), F32),
            pltpu.VMEM((chunks, planes, 2, rows, chunk), BF16),
            pltpu.VMEM((chunks, 2 * tok, chunk), BF16),
            pltpu.VMEM((planes, 2, HEAD_DIM, width), BF16),
            pltpu.VMEM((planes, 2, HEAD_DIM, width), BF16),
            pltpu.VMEM((planes, 2, tok, width), BF16),
            pltpu.VMEM((planes, 2, 2, tok, width), BF16),
            pltpu.VMEM((planes, 4 * tok, width), BF16),
            pltpu.VMEM((planes, 2, tok, width), F32),
            pltpu.VMEM((2, tok, 128), F32),
            pltpu.VMEM((chunks, 2, 2 * tok, chunk), F32),
            pltpu.VMEM((chunks, 2 * tok, chunk), BF16),
            pltpu.VMEM((chunks, 2 * tok, chunk), BF16),
            dma((chunks,)),
            dma((chunks, planes, 3)),
            dma((chunks, planes, 2)),
            dma((planes, 2)),
            dma((planes, 2)),
            dma((planes, 2, 2)),
            dma((planes, 2, 2)),
            dma,
            dma,
            dma((chunks,)),
            dma((chunks,)),
            dma((4,)),
            dma((chunks,)),
        ],
        compiler_params=pltpu.CompilerParams(
            collective_id=0, has_side_effects=True, vmem_limit_bytes=56 * 1024 * 1024
        ),
    )(queries, keys, values, norm_gain.reshape(1, features), out_weight)


def solution(mesh):
    placed = (
        P(("fsdp", "ctx"), None),
        P(("fsdp", "ctx"), None),
        P(("fsdp", "ctx"), None),
        P(),
        P("fsdp", "ctx"),
    )
    planes = mesh.shape["fsdp"] // 4
    chunks = planes

    def body(queries, keys, values, norm_gain, out_weight):
        rows, out_columns = out_weight.shape
        width = 2 * rows
        fits = (
            mesh.shape["ctx"] == 2
            and mesh.shape["fsdp"] == 4 * planes
            and planes == 4
            and rows % 16 == 0
            and width % HEAD_DIM == 0
            and width % 128 == 0
            and out_columns % (128 * chunks) == 0
        )
        if fits:
            return fused(planes, chunks, queries, keys, values, norm_gain, out_weight)
        return on_device(queries, keys, values, norm_gain, out_weight)

    return jax.shard_map(
        body, mesh=mesh, in_specs=placed, out_specs=P("fsdp", "ctx"), check_vma=False
    )
```

```python
import functools

import jax
import jax.numpy as jnp
from jax import lax
from jax.experimental import pallas as pl
from jax.experimental.pallas import tpu as pltpu
from jax.sharding import PartitionSpec as P

HEADS = 32
HEAD_DIM = 96
MESH = pl.DeviceIdType.MESH
BF16 = jnp.bfloat16
F32 = jnp.float32


def on_device(queries, keys, values, norm_gain, out_weight):
    tok_rows = queries.shape[0]
    q_heads = queries.reshape(tok_rows, HEADS, HEAD_DIM)
    k_heads = keys.reshape(tok_rows, HEADS, HEAD_DIM)
    v_heads = values.reshape(tok_rows, HEADS, HEAD_DIM)
    scores = jnp.einsum("thd,shd->hts", q_heads, k_heads, preferred_element_type=jnp.float32)
    causal = jnp.arange(tok_rows)[:, None] >= jnp.arange(tok_rows)[None, :]
    scores = jnp.where(causal, scores, 0.0).astype(jnp.bfloat16)
    intra = jnp.einsum("hts,shd->thd", scores, v_heads, preferred_element_type=jnp.float32)
    local_state = jnp.einsum("shd,she->hde", k_heads, v_heads, preferred_element_type=jnp.float32)
    flat_state = local_state.reshape(HEADS, HEAD_DIM * HEAD_DIM).astype(jnp.bfloat16)
    every_state = lax.all_gather(flat_state[None], "ctx", axis=0, tiled=True)
    position = lax.axis_index("ctx")
    earlier = (jnp.arange(every_state.shape[0]) < position)[:, None, None]
    prefix_flat = jnp.sum(jnp.where(earlier, every_state.astype(jnp.float32), 0.0), axis=0)
    prefix_state = prefix_flat.reshape(HEADS, HEAD_DIM, HEAD_DIM).astype(jnp.bfloat16)
    inter = jnp.einsum("thd,hde->the", q_heads, prefix_state, preferred_element_type=jnp.float32)
    attn = (intra + inter).reshape(tok_rows, HEADS * HEAD_DIM)
    mean_sq = jnp.mean(attn * attn, axis=-1, keepdims=True)
    normed = (attn * lax.rsqrt(mean_sq + 1e-05) * norm_gain).astype(jnp.bfloat16)
    weight_block = lax.all_gather(out_weight, "fsdp", axis=0, tiled=True)
    result = jnp.dot(
        lax.all_gather(normed, "ctx", axis=0, tiled=True),
        weight_block,
        preferred_element_type=jnp.float32,
    )
    return result.astype(jnp.bfloat16)


def kernel(
    planes, chunks, q_in, k_in, v_in, gain_in, w_ref, out_ref,
    q_ref, k_ref, v_ref, gain_ref, w_all, state_own, state_in, x_out, x_all, x_cat, att, ms, acc, part_out, part_in,
    w_load, w_send, w_recv, state_send, state_recv, x_send, x_recv, ms_send, ms_recv,
    part_send, part_recv, in_load,
):
    tok, features = q_ref.shape
    rows = w_ref.shape[0]
    width = 2 * rows
    chunk = w_ref.shape[1] // chunks
    group_heads = width // HEAD_DIM

    f = lax.axis_index("fsdp")
    x = lax.axis_index("ctx")
    z, y, c = lax.div(f, 4), lax.rem(lax.div(f, 2), 2), lax.rem(f, 2)

    def at(zz, yy, cc, xx):
        return (4 * zz + 2 * yy + cc, xx)

    sibling = at(z, y, 1 - c, x)
    far_end = at(planes - 1 - z, y, c, x)
    at_end = (z == 0) | (z == planes - 1)
    across = at(z, y, c, 1 - x)
    beside = at(z, 1 - y, c, x)
    diagonal = at(z, 1 - y, c, 1 - x)

    def remote(src, dst, send, recv, device):
        return pltpu.make_async_remote_copy(
            src_ref=src, dst_ref=dst, send_sem=send, recv_sem=recv,
            device_id=device, device_id_type=MESH,
        )

    def load(j):
        return pltpu.make_async_copy(
            w_ref.at[:, pl.ds(pl.multiple_of(j * chunk, chunk), chunk)],
            w_all.at[j, z, c], w_load.at[j],
        )

    def w_copy(j, plane, way):
        device = (at(z - 1, y, c, x), at(z + 1, y, c, x), sibling, far_end)[way]
        block = w_all.at[j, plane, c]
        return remote(block, block, w_send.at[j, plane, way], w_recv.at[j, plane, c], device)

    def w_arrive(j, plane, core):
        block = w_all.at[j, plane, core]
        remote(block, block, w_send.at[j, plane, 2], w_recv.at[j, plane, core], sibling).wait_recv()

    def each(body, count=planes):
        def step(i, carry):
            body(i)
            return carry
        lax.fori_loop(0, count, step, 0)

    every_chunk = functools.partial(each, count=chunks)
    every_chunk(lambda j: load(j).start())
    inputs = [
        pltpu.make_async_copy(src, dst, in_load.at[n])
        for n, (src, dst) in enumerate(
            ((k_in, k_ref), (v_in, v_ref), (q_in, q_ref), (gain_in, gain_ref))
        )
    ]
    for copy in inputs:
        copy.start()

    barrier = pltpu.get_barrier_semaphore()
    for device in (sibling, across, beside, diagonal):
        pl.semaphore_signal(barrier, inc=1, device_id=device, device_id_type=MESH)

    @pl.when(z > 0)
    def _():
        pl.semaphore_signal(barrier, inc=1, device_id=at(z - 1, y, c, x), device_id_type=MESH)

    @pl.when(z < planes - 1)
    def _():
        pl.semaphore_signal(barrier, inc=1, device_id=at(z + 1, y, c, x), device_id_type=MESH)

    @pl.when(at_end)
    def _():
        pl.semaphore_signal(barrier, inc=1, device_id=far_end, device_id_type=MESH)

    pl.semaphore_wait(barrier, 4 + jnp.where(at_end, 1, 0) + jnp.where(z > 0, 1, 0) + jnp.where(z < planes - 1, 1, 0))

    def send_own(j):
        load(j).wait()

        @pl.when(z > 0)
        def _():
            w_copy(j, z, 0).start()

        @pl.when(z < planes - 1)
        def _():
            w_copy(j, z, 1).start()

        w_copy(j, z, 2).start()

        @pl.when(at_end)
        def _():
            w_copy(j, z, 3).start()

    every_chunk(send_own)
    for copy in inputs:
        copy.wait()

    lane = lax.broadcasted_iota(jnp.int32, (1, width), 1)
    in_head = [
        jnp.where((lane >= h * HEAD_DIM) & (lane < (h + 1) * HEAD_DIM), 1.0, 0.0)
        for h in range(group_heads)
    ]
    in_head16 = [m.astype(BF16) for m in in_head]

    def columns(i, yy):
        return pl.ds(pl.multiple_of(i * (2 * width), 2 * width) + yy * width, width)

    def state_copy(i, yy):
        return remote(
            state_own.at[i, yy], state_in.at[i, yy], state_send.at[i, yy], state_recv.at[i, yy], across
        )

    @pl.when(x == 0)
    def _():
        def states(i):
            for yy in range(2):
                full = lax.dot_general(
                    k_ref[:, columns(i, yy)], v_ref[:, columns(i, yy)],
                    (((0,), (0,)), ((), ())), preferred_element_type=F32,
                )
                folded = full[:HEAD_DIM] * in_head[0]
                for h in range(1, group_heads):
                    folded = folded + full[h * HEAD_DIM:(h + 1) * HEAD_DIM] * in_head[h]
                state_own[i, yy] = folded.astype(BF16)
                state_copy(i, yy).start()
        each(states)

    def pass_on(j, distance):
        @pl.when(z - distance >= 0)
        def _():
            w_arrive(j, z - distance, c)
            if distance == 1:
                @pl.when(z < planes - 1)
                def _():
                    w_copy(j, z - 1, 1).start()

            w_copy(j, z - distance, 2).start()

        @pl.when(z + distance < planes)
        def _():
            w_arrive(j, z + distance, c)
            if distance == 1:
                @pl.when(z > 0)
                def _():
                    w_copy(j, z + 1, 0).start()

            w_copy(j, z + distance, 2).start()

    def x_near(i, yy):
        return remote(
            x_out.at[i, yy], x_all.at[i, y, x], x_send.at[i, yy, 0], x_recv.at[i, y, x], at(z, yy, c, x)
        )

    def x_far(i, yy):
        return remote(
            x_out.at[i, yy], x_all.at[i, y, x], x_send.at[i, yy, 1], x_recv.at[i, y, x],
            at(z, yy, c, 1 - x),
        )

    causal = (
        lax.broadcasted_iota(jnp.int32, (tok, tok), 0) >= lax.broadcasted_iota(jnp.int32, (tok, tok), 1)
    )
    ms[x] = jnp.zeros(ms.shape[1:], F32)

    def deliver(i, yy, attn):
        ms[x] += jnp.broadcast_to(
            jnp.sum(attn * attn, axis=-1, keepdims=True) * (1.0 / features), ms.shape[1:]
        )
        scaled = (attn * gain_ref[:, columns(i, yy)]).astype(BF16)
        x_out[i, yy] = scaled
        x_far(i, yy).start()

        @pl.when(y != yy)
        def _():
            x_near(i, yy).start()

        @pl.when(y == yy)
        def _():
            x_all[i, y, x] = scaled

    def attend(i):
        for yy in range(2):
            q, k, v = (ref[:, columns(i, yy)] for ref in (q_ref, k_ref, v_ref))
            total = jnp.zeros((tok, width), F32)
            for h in range(group_heads):
                scores = lax.dot_general(
                    q * in_head16[h], k, (((1,), (1,)), ((), ())), preferred_element_type=F32
                )
                scores = jnp.where(causal, scores, 0.0).astype(BF16)
                total = total + jnp.dot(scores, v * in_head16[h], preferred_element_type=F32)
            att[i, yy] = total

            @pl.when(x == 0)
            def _():
                deliver(i, yy, att[i, yy])

        pass_on(i, 1)

    each(attend)
    for j in range(planes, chunks):
        pass_on(j, 1)

    def attend_earlier(i):
        @pl.when(x == 1)
        def _():
            for yy in range(2):
                state_copy(i, yy).wait_recv()
                state = state_in[i, yy]
                wide = jnp.concatenate([state * m for m in in_head16], axis=0)
                inter = jnp.dot(q_ref[:, columns(i, yy)], wide, preferred_element_type=F32)
                deliver(i, yy, att[i, yy] + inter)

    each(attend_earlier)
    ms_copy = remote(ms.at[x], ms.at[x], ms_send, ms_recv, across)
    ms_copy.start()

    def x_arrive(i, yy, xx):
        remote(
            x_all.at[i, yy, xx], x_all.at[i, yy, xx], x_send.at[i, yy, 1], x_recv.at[i, yy, xx], across
        ).wait_recv()

    def merge(i):
        x_arrive(i, y, 1 - x)
        x_arrive(i, 1 - y, x)
        x_arrive(i, 1 - y, 1 - x)
        parts = [x_all[i, yy, xx].astype(F32) for yy in range(2) for xx in range(2)]
        x_cat[i] = jnp.concatenate(parts, axis=0).astype(BF16)

    each(merge)

    def multiply(j, plane):
        w_arrive(j, plane, 1 - c)
        return jnp.dot(
            x_cat[plane], w_all[j, plane].reshape(width, chunk), preferred_element_type=F32
        )

    def first(j):
        total = multiply(j, z)
        acc[j, 0] = total[:2 * tok]
        acc[j, 1] = total[2 * tok:]

    every_chunk(first)

    def add(j, plane):
        total = multiply(j, plane)
        acc[j, 0] += total[:2 * tok]
        acc[j, 1] += total[2 * tok:]

    def add_both(j, distance):
        @pl.when(z - distance >= 0)
        def _():
            add(j, z - distance)

        @pl.when(z + distance < planes)
        def _():
            add(j, z + distance)

    every_chunk(functools.partial(add_both, distance=1))

    def part_copy(j):
        return remote(part_out.at[j], part_in.at[j], part_send.at[j], part_recv.at[j], beside)

    def last(j):
        for distance in range(2, planes):
            pass_on(j, distance)
        for distance in range(2, planes):
            add_both(j, distance)
        part_out[j] = acc[j, 1 - y].astype(BF16)
        part_copy(j).start()

    every_chunk(last)

    remote(ms.at[1 - x], ms.at[1 - x], ms_send, ms_recv, across).wait_recv()
    mean_sq = jnp.concatenate([ms[0][:, :1], ms[1][:, :1]], axis=0)
    scale = lax.rsqrt(mean_sq + 1e-05)

    def finish(j):
        part_copy(j).wait_recv()
        total = acc[j, y] + part_in[j].astype(F32)
        out_ref[:, pl.ds(pl.multiple_of(j * chunk, chunk), chunk)] = (total * scale).astype(BF16)

    every_chunk(finish)

    def drain(i):
        for yy in range(2):
            x_far(i, yy).wait_send()

            @pl.when(y != yy)
            def _():
                x_near(i, yy).wait_send()

            @pl.when(x == 0)
            def _():
                state_copy(i, yy).wait_send()

    def drain_chunk(i):
        part_copy(i).wait_send()

        for plane in range(planes):
            w_copy(i, plane, 2).wait_send()

            @pl.when(((plane == z) | (plane == z + 1)) & (z > 0))
            def _():
                w_copy(i, plane, 0).wait_send()

            @pl.when(((plane == z) | (plane == z - 1)) & (z < planes - 1))
            def _():
                w_copy(i, plane, 1).wait_send()

        @pl.when(at_end)
        def _():
            w_copy(i, z, 3).wait_send()

    each(drain)
    every_chunk(drain_chunk)
    ms_copy.wait_send()


def fused(planes, chunks, queries, keys, values, norm_gain, out_weight):
    tok, features = queries.shape
    rows, out_columns = out_weight.shape
    width, chunk = 2 * rows, out_columns // chunks
    anywhere = pl.BlockSpec(memory_space=pl.ANY)
    dma = pltpu.SemaphoreType.DMA
    return pl.pallas_call(
        functools.partial(kernel, planes, chunks),
        out_shape=jax.ShapeDtypeStruct((2 * tok, out_columns), BF16),
        in_specs=[anywhere] * 5,
        out_specs=pl.BlockSpec(memory_space=pltpu.VMEM),
        scratch_shapes=[
            pltpu.VMEM((tok, features), BF16),
            pltpu.VMEM((tok, features), BF16),
            pltpu.VMEM((tok, features), BF16),
            pltpu.VMEM((1, features), F32),
            pltpu.VMEM((chunks, planes, 2, rows, chunk), BF16),
            pltpu.VMEM((planes, 2, HEAD_DIM, width), BF16),
            pltpu.VMEM((planes, 2, HEAD_DIM, width), BF16),
            pltpu.VMEM((planes, 2, tok, width), BF16),
            pltpu.VMEM((planes, 2, 2, tok, width), BF16),
            pltpu.VMEM((planes, 4 * tok, width), BF16),
            pltpu.VMEM((planes, 2, tok, width), F32),
            pltpu.VMEM((2, tok, 128), F32),
            pltpu.VMEM((chunks, 2, 2 * tok, chunk), F32),
            pltpu.VMEM((chunks, 2 * tok, chunk), BF16),
            pltpu.VMEM((chunks, 2 * tok, chunk), BF16),
            dma((chunks,)),
            dma((chunks, planes, 4)),
            dma((chunks, planes, 2)),
            dma((planes, 2)),
            dma((planes, 2)),
            dma((planes, 2, 2)),
            dma((planes, 2, 2)),
            dma,
            dma,
            dma((chunks,)),
            dma((chunks,)),
            dma((4,)),
        ],
        compiler_params=pltpu.CompilerParams(
            collective_id=0, has_side_effects=True, vmem_limit_bytes=48 * 1024 * 1024
        ),
    )(queries, keys, values, norm_gain.reshape(1, features), out_weight)


def solution(mesh):
    placed = (
        P(("fsdp", "ctx"), None),
        P(("fsdp", "ctx"), None),
        P(("fsdp", "ctx"), None),
        P(),
        P("fsdp", "ctx"),
    )
    planes = mesh.shape["fsdp"] // 4
    chunks = 6

    def body(queries, keys, values, norm_gain, out_weight):
        rows, out_columns = out_weight.shape
        width = 2 * rows
        fits = (
            mesh.shape["ctx"] == 2
            and mesh.shape["fsdp"] == 4 * planes
            and planes == 4
            and rows % 16 == 0
            and width % HEAD_DIM == 0
            and width % 128 == 0
            and out_columns % (128 * chunks) == 0
        )
        if fits:
            return fused(planes, chunks, queries, keys, values, norm_gain, out_weight)
        return on_device(queries, keys, values, norm_gain, out_weight)

    return jax.shard_map(
        body, mesh=mesh, in_specs=placed, out_specs=P("fsdp", "ctx"), check_vma=False
    )
```

```python
import functools

import jax
import jax.numpy as jnp
from jax import lax
from jax.experimental import pallas as pl
from jax.experimental.pallas import tpu as pltpu
from jax.sharding import PartitionSpec as P

HEADS = 32
HEAD_DIM = 96
MESH = pl.DeviceIdType.MESH
BF16 = jnp.bfloat16
F32 = jnp.float32


def on_device(queries, keys, values, norm_gain, out_weight):
    tok_rows = queries.shape[0]
    q_heads = queries.reshape(tok_rows, HEADS, HEAD_DIM)
    k_heads = keys.reshape(tok_rows, HEADS, HEAD_DIM)
    v_heads = values.reshape(tok_rows, HEADS, HEAD_DIM)
    scores = jnp.einsum("thd,shd->hts", q_heads, k_heads, preferred_element_type=jnp.float32)
    causal = jnp.arange(tok_rows)[:, None] >= jnp.arange(tok_rows)[None, :]
    scores = jnp.where(causal, scores, 0.0).astype(jnp.bfloat16)
    intra = jnp.einsum("hts,shd->thd", scores, v_heads, preferred_element_type=jnp.float32)
    local_state = jnp.einsum("shd,she->hde", k_heads, v_heads, preferred_element_type=jnp.float32)
    flat_state = local_state.reshape(HEADS, HEAD_DIM * HEAD_DIM).astype(jnp.bfloat16)
    every_state = lax.all_gather(flat_state[None], "ctx", axis=0, tiled=True)
    position = lax.axis_index("ctx")
    earlier = (jnp.arange(every_state.shape[0]) < position)[:, None, None]
    prefix_flat = jnp.sum(jnp.where(earlier, every_state.astype(jnp.float32), 0.0), axis=0)
    prefix_state = prefix_flat.reshape(HEADS, HEAD_DIM, HEAD_DIM).astype(jnp.bfloat16)
    inter = jnp.einsum("thd,hde->the", q_heads, prefix_state, preferred_element_type=jnp.float32)
    attn = (intra + inter).reshape(tok_rows, HEADS * HEAD_DIM)
    mean_sq = jnp.mean(attn * attn, axis=-1, keepdims=True)
    normed = (attn * lax.rsqrt(mean_sq + 1e-05) * norm_gain).astype(jnp.bfloat16)
    weight_block = lax.all_gather(out_weight, "fsdp", axis=0, tiled=True)
    result = jnp.dot(
        lax.all_gather(normed, "ctx", axis=0, tiled=True),
        weight_block,
        preferred_element_type=jnp.float32,
    )
    return result.astype(jnp.bfloat16)


def kernel(
    planes, chunks, q_in, k_in, v_in, gain_in, w_ref, out_ref,
    q_ref, k_ref, v_ref, gain_ref, w_all, state_own, state_in, x_out, x_all, x_cat, att, ms, acc, part_out, part_in,
    w_load, w_send, w_recv, state_send, state_recv, x_send, x_recv, ms_send, ms_recv,
    part_send, part_recv, in_load,
):
    tok, features = q_ref.shape
    rows = w_ref.shape[0]
    width = 2 * rows
    chunk = w_ref.shape[1] // chunks
    group_heads = width // HEAD_DIM

    f = lax.axis_index("fsdp")
    x = lax.axis_index("ctx")
    z, y, c = lax.div(f, 4), lax.rem(lax.div(f, 2), 2), lax.rem(f, 2)

    def at(zz, yy, cc, xx):
        return (4 * zz + 2 * yy + cc, xx)

    sibling = at(z, y, 1 - c, x)
    across = at(z, y, c, 1 - x)
    beside = at(z, 1 - y, c, x)
    diagonal = at(z, 1 - y, c, 1 - x)

    def remote(src, dst, send, recv, device):
        return pltpu.make_async_remote_copy(
            src_ref=src, dst_ref=dst, send_sem=send, recv_sem=recv,
            device_id=device, device_id_type=MESH,
        )

    def load(j):
        return pltpu.make_async_copy(
            w_ref.at[:, pl.ds(pl.multiple_of(j * chunk, chunk), chunk)],
            w_all.at[j, z, c], w_load.at[j],
        )

    def w_copy(j, plane, way):
        device = (at(z - 1, y, c, x), at(z + 1, y, c, x), sibling)[way]
        block = w_all.at[j, plane, c]
        return remote(block, block, w_send.at[j, plane, way], w_recv.at[j, plane, c], device)

    def w_arrive(j, plane, core):
        block = w_all.at[j, plane, core]
        remote(block, block, w_send.at[j, plane, 2], w_recv.at[j, plane, core], sibling).wait_recv()

    def each(body, count=planes):
        def step(i, carry):
            body(i)
            return carry
        lax.fori_loop(0, count, step, 0)

    every_chunk = functools.partial(each, count=chunks)
    every_chunk(lambda j: load(j).start())
    inputs = [
        pltpu.make_async_copy(src, dst, in_load.at[n])
        for n, (src, dst) in enumerate(
            ((k_in, k_ref), (v_in, v_ref), (q_in, q_ref), (gain_in, gain_ref))
        )
    ]
    for copy in inputs:
        copy.start()

    barrier = pltpu.get_barrier_semaphore()
    for device in (sibling, across, beside, diagonal):
        pl.semaphore_signal(barrier, inc=1, device_id=device, device_id_type=MESH)

    @pl.when(z > 0)
    def _():
        pl.semaphore_signal(barrier, inc=1, device_id=at(z - 1, y, c, x), device_id_type=MESH)

    @pl.when(z < planes - 1)
    def _():
        pl.semaphore_signal(barrier, inc=1, device_id=at(z + 1, y, c, x), device_id_type=MESH)

    pl.semaphore_wait(barrier, 4 + jnp.where(z > 0, 1, 0) + jnp.where(z < planes - 1, 1, 0))

    def send_own(j):
        load(j).wait()

        @pl.when(z > 0)
        def _():
            w_copy(j, z, 0).start()

        @pl.when(z < planes - 1)
        def _():
            w_copy(j, z, 1).start()

        w_copy(j, z, 2).start()

    every_chunk(send_own)
    for copy in inputs:
        copy.wait()

    lane = lax.broadcasted_iota(jnp.int32, (1, width), 1)
    in_head = [
        jnp.where((lane >= h * HEAD_DIM) & (lane < (h + 1) * HEAD_DIM), 1.0, 0.0)
        for h in range(group_heads)
    ]
    in_head16 = [m.astype(BF16) for m in in_head]

    def columns(i, yy):
        return pl.ds(pl.multiple_of(i * (2 * width), 2 * width) + yy * width, width)

    def state_copy(i, yy):
        return remote(
            state_own.at[i, yy], state_in.at[i, yy], state_send.at[i, yy], state_recv.at[i, yy], across
        )

    @pl.when(x == 0)
    def _():
        def states(i):
            for yy in range(2):
                full = lax.dot_general(
                    k_ref[:, columns(i, yy)], v_ref[:, columns(i, yy)],
                    (((0,), (0,)), ((), ())), preferred_element_type=F32,
                )
                folded = full[:HEAD_DIM] * in_head[0]
                for h in range(1, group_heads):
                    folded = folded + full[h * HEAD_DIM:(h + 1) * HEAD_DIM] * in_head[h]
                state_own[i, yy] = folded.astype(BF16)
                state_copy(i, yy).start()
        each(states)

    def pass_on(j, distance):
        @pl.when(z - distance >= 0)
        def _():
            w_arrive(j, z - distance, c)

            @pl.when(z < planes - 1)
            def _():
                w_copy(j, z - distance, 1).start()

            w_copy(j, z - distance, 2).start()

        @pl.when(z + distance < planes)
        def _():
            w_arrive(j, z + distance, c)

            @pl.when(z > 0)
            def _():
                w_copy(j, z + distance, 0).start()

            w_copy(j, z + distance, 2).start()

    def x_near(i, yy):
        return remote(
            x_out.at[i, yy], x_all.at[i, y, x], x_send.at[i, yy, 0], x_recv.at[i, y, x], at(z, yy, c, x)
        )

    def x_far(i, yy):
        return remote(
            x_out.at[i, yy], x_all.at[i, y, x], x_send.at[i, yy, 1], x_recv.at[i, y, x],
            at(z, yy, c, 1 - x),
        )

    causal = (
        lax.broadcasted_iota(jnp.int32, (tok, tok), 0) >= lax.broadcasted_iota(jnp.int32, (tok, tok), 1)
    )
    ms[x] = jnp.zeros(ms.shape[1:], F32)

    def deliver(i, yy, attn):
        ms[x] += jnp.broadcast_to(
            jnp.sum(attn * attn, axis=-1, keepdims=True) * (1.0 / features), ms.shape[1:]
        )
        scaled = (attn * gain_ref[:, columns(i, yy)]).astype(BF16)
        x_out[i, yy] = scaled

        @pl.when(y != yy)
        def _():
            x_near(i, yy).start()

        @pl.when(y == yy)
        def _():
            x_all[i, y, x] = scaled

    def attend(i):
        for yy in range(2):
            q, k, v = (ref[:, columns(i, yy)] for ref in (q_ref, k_ref, v_ref))
            total = jnp.zeros((tok, width), F32)
            for h in range(group_heads):
                scores = lax.dot_general(
                    q * in_head16[h], k, (((1,), (1,)), ((), ())), preferred_element_type=F32
                )
                scores = jnp.where(causal, scores, 0.0).astype(BF16)
                total = total + jnp.dot(scores, v * in_head16[h], preferred_element_type=F32)
            att[i, yy] = total

            @pl.when(x == 0)
            def _():
                deliver(i, yy, att[i, yy])

        pass_on(i, 1)

    each(attend)
    for j in range(planes, chunks):
        pass_on(j, 1)

    @pl.when(x == 0)
    def _():
        def states_sent(i):
            for yy in range(2):
                state_copy(i, yy).wait_send()
        each(states_sent)

    def attend_earlier(i):
        @pl.when(x == 1)
        def _():
            for yy in range(2):
                state_copy(i, yy).wait_recv()
                state = state_in[i, yy]
                wide = jnp.concatenate([state * m for m in in_head16], axis=0)
                inter = jnp.dot(q_ref[:, columns(i, yy)], wide, preferred_element_type=F32)
                deliver(i, yy, att[i, yy] + inter)

        for yy in range(2):
            x_far(i, yy).start()
        pass_on(i, 2)

    each(attend_earlier)
    for j in range(planes, chunks):
        pass_on(j, 2)
    ms_copy = remote(ms.at[x], ms.at[x], ms_send, ms_recv, across)
    ms_copy.start()

    def x_arrive(i, yy, xx):
        remote(
            x_all.at[i, yy, xx], x_all.at[i, yy, xx], x_send.at[i, yy, 1], x_recv.at[i, yy, xx], across
        ).wait_recv()

    def merge(i):
        x_arrive(i, y, 1 - x)
        x_arrive(i, 1 - y, x)
        x_arrive(i, 1 - y, 1 - x)
        parts = [x_all[i, yy, xx].astype(F32) for yy in range(2) for xx in range(2)]
        x_cat[i] = jnp.concatenate(parts, axis=0).astype(BF16)

    each(merge)

    def multiply(j, plane):
        w_arrive(j, plane, 1 - c)
        return jnp.dot(
            x_cat[plane], w_all[j, plane].reshape(width, chunk), preferred_element_type=F32
        )

    def first(j):
        total = multiply(j, z)
        acc[j, 0] = total[:2 * tok]
        acc[j, 1] = total[2 * tok:]

    every_chunk(first)

    def add(j, plane):
        total = multiply(j, plane)
        acc[j, 0] += total[:2 * tok]
        acc[j, 1] += total[2 * tok:]

    def add_both(j, distance):
        @pl.when(z - distance >= 0)
        def _():
            add(j, z - distance)

        @pl.when(z + distance < planes)
        def _():
            add(j, z + distance)

    for distance in range(1, planes - 1):
        every_chunk(functools.partial(add_both, distance=distance))

    def part_copy(j):
        return remote(part_out.at[j], part_in.at[j], part_send.at[j], part_recv.at[j], beside)

    def last(j):
        pass_on(j, planes - 1)
        add_both(j, planes - 1)
        part_out[j] = acc[j, 1 - y].astype(BF16)
        part_copy(j).start()

    every_chunk(last)

    remote(ms.at[1 - x], ms.at[1 - x], ms_send, ms_recv, across).wait_recv()
    mean_sq = jnp.concatenate([ms[0][:, :1], ms[1][:, :1]], axis=0)
    scale = lax.rsqrt(mean_sq + 1e-05)

    def finish(j):
        part_copy(j).wait_recv()
        total = acc[j, y] + part_in[j].astype(F32)
        out_ref[:, pl.ds(pl.multiple_of(j * chunk, chunk), chunk)] = (total * scale).astype(BF16)

    every_chunk(finish)

    def drain(i):
        for yy in range(2):
            x_far(i, yy).wait_send()

            @pl.when(y != yy)
            def _():
                x_near(i, yy).wait_send()

    def drain_chunk(i):
        part_copy(i).wait_send()

        for plane in range(planes):
            w_copy(i, plane, 2).wait_send()

            @pl.when((plane >= z) & (z > 0))
            def _():
                w_copy(i, plane, 0).wait_send()

            @pl.when((plane <= z) & (z < planes - 1))
            def _():
                w_copy(i, plane, 1).wait_send()

    each(drain)
    every_chunk(drain_chunk)
    ms_copy.wait_send()


def fused(planes, chunks, queries, keys, values, norm_gain, out_weight):
    tok, features = queries.shape
    rows, out_columns = out_weight.shape
    width, chunk = 2 * rows, out_columns // chunks
    anywhere = pl.BlockSpec(memory_space=pl.ANY)
    dma = pltpu.SemaphoreType.DMA
    return pl.pallas_call(
        functools.partial(kernel, planes, chunks),
        out_shape=jax.ShapeDtypeStruct((2 * tok, out_columns), BF16),
        in_specs=[anywhere] * 5,
        out_specs=pl.BlockSpec(memory_space=pltpu.VMEM),
        scratch_shapes=[
            pltpu.VMEM((tok, features), BF16),
            pltpu.VMEM((tok, features), BF16),
            pltpu.VMEM((tok, features), BF16),
            pltpu.VMEM((1, features), F32),
            pltpu.VMEM((chunks, planes, 2, rows, chunk), BF16),
            pltpu.VMEM((planes, 2, HEAD_DIM, width), BF16),
            pltpu.VMEM((planes, 2, HEAD_DIM, width), BF16),
            pltpu.VMEM((planes, 2, tok, width), BF16),
            pltpu.VMEM((planes, 2, 2, tok, width), BF16),
            pltpu.VMEM((planes, 4 * tok, width), BF16),
            pltpu.VMEM((planes, 2, tok, width), F32),
            pltpu.VMEM((2, tok, 128), F32),
            pltpu.VMEM((chunks, 2, 2 * tok, chunk), F32),
            pltpu.VMEM((chunks, 2 * tok, chunk), BF16),
            pltpu.VMEM((chunks, 2 * tok, chunk), BF16),
            dma((chunks,)),
            dma((chunks, planes, 3)),
            dma((chunks, planes, 2)),
            dma((planes, 2)),
            dma((planes, 2)),
            dma((planes, 2, 2)),
            dma((planes, 2, 2)),
            dma,
            dma,
            dma((chunks,)),
            dma((chunks,)),
            dma((4,)),
        ],
        compiler_params=pltpu.CompilerParams(
            collective_id=0, has_side_effects=True, vmem_limit_bytes=56 * 1024 * 1024
        ),
    )(queries, keys, values, norm_gain.reshape(1, features), out_weight)


def solution(mesh):
    placed = (
        P(("fsdp", "ctx"), None),
        P(("fsdp", "ctx"), None),
        P(("fsdp", "ctx"), None),
        P(),
        P("fsdp", "ctx"),
    )
    planes = mesh.shape["fsdp"] // 4
    chunks = 6

    def body(queries, keys, values, norm_gain, out_weight):
        rows, out_columns = out_weight.shape
        width = 2 * rows
        fits = (
            mesh.shape["ctx"] == 2
            and mesh.shape["fsdp"] == 4 * planes
            and planes == 4
            and rows % 16 == 0
            and width % HEAD_DIM == 0
            and width % 128 == 0
            and out_columns % (128 * chunks) == 0
        )
        if fits:
            return fused(planes, chunks, queries, keys, values, norm_gain, out_weight)
        return on_device(queries, keys, values, norm_gain, out_weight)

    return jax.shard_map(
        body, mesh=mesh, in_specs=placed, out_specs=P("fsdp", "ctx"), check_vma=False
    )
```

```python
import functools

import jax
import jax.numpy as jnp
from jax import lax
from jax.experimental import pallas as pl
from jax.experimental.pallas import tpu as pltpu
from jax.sharding import PartitionSpec as P

HEADS = 32
HEAD_DIM = 96
MESH = pl.DeviceIdType.MESH
BF16 = jnp.bfloat16
F32 = jnp.float32


def on_device(queries, keys, values, norm_gain, out_weight):
    tok_rows = queries.shape[0]
    q_heads = queries.reshape(tok_rows, HEADS, HEAD_DIM)
    k_heads = keys.reshape(tok_rows, HEADS, HEAD_DIM)
    v_heads = values.reshape(tok_rows, HEADS, HEAD_DIM)
    scores = jnp.einsum("thd,shd->hts", q_heads, k_heads, preferred_element_type=jnp.float32)
    causal = jnp.arange(tok_rows)[:, None] >= jnp.arange(tok_rows)[None, :]
    scores = jnp.where(causal, scores, 0.0).astype(jnp.bfloat16)
    intra = jnp.einsum("hts,shd->thd", scores, v_heads, preferred_element_type=jnp.float32)
    local_state = jnp.einsum("shd,she->hde", k_heads, v_heads, preferred_element_type=jnp.float32)
    flat_state = local_state.reshape(HEADS, HEAD_DIM * HEAD_DIM).astype(jnp.bfloat16)
    every_state = lax.all_gather(flat_state[None], "ctx", axis=0, tiled=True)
    position = lax.axis_index("ctx")
    earlier = (jnp.arange(every_state.shape[0]) < position)[:, None, None]
    prefix_flat = jnp.sum(jnp.where(earlier, every_state.astype(jnp.float32), 0.0), axis=0)
    prefix_state = prefix_flat.reshape(HEADS, HEAD_DIM, HEAD_DIM).astype(jnp.bfloat16)
    inter = jnp.einsum("thd,hde->the", q_heads, prefix_state, preferred_element_type=jnp.float32)
    attn = (intra + inter).reshape(tok_rows, HEADS * HEAD_DIM)
    mean_sq = jnp.mean(attn * attn, axis=-1, keepdims=True)
    normed = (attn * lax.rsqrt(mean_sq + 1e-05) * norm_gain).astype(jnp.bfloat16)
    weight_block = lax.all_gather(out_weight, "fsdp", axis=0, tiled=True)
    result = jnp.dot(
        lax.all_gather(normed, "ctx", axis=0, tiled=True),
        weight_block,
        preferred_element_type=jnp.float32,
    )
    return result.astype(jnp.bfloat16)


def kernel(
    planes, chunks, q_in, k_in, v_in, gain_in, w_ref, out_ref,
    q_ref, k_ref, v_ref, gain_ref, w_all, state_own, state_in, x_out, x_all, x_cat, att, ms, acc, part_out, part_in,
    w_load, w_send, w_recv, state_send, state_recv, x_send, x_recv, ms_send, ms_recv,
    part_send, part_recv, in_load,
):
    tok, features = q_ref.shape
    rows = w_ref.shape[0]
    width = 2 * rows
    chunk = w_ref.shape[1] // chunks
    group_heads = width // HEAD_DIM

    f = lax.axis_index("fsdp")
    x = lax.axis_index("ctx")
    z, y, c = lax.div(f, 4), lax.rem(lax.div(f, 2), 2), lax.rem(f, 2)

    def at(zz, yy, cc, xx):
        return (4 * zz + 2 * yy + cc, xx)

    sibling = at(z, y, 1 - c, x)
    across = at(z, y, c, 1 - x)
    beside = at(z, 1 - y, c, x)
    diagonal = at(z, 1 - y, c, 1 - x)

    def remote(src, dst, send, recv, device):
        return pltpu.make_async_remote_copy(
            src_ref=src, dst_ref=dst, send_sem=send, recv_sem=recv,
            device_id=device, device_id_type=MESH,
        )

    def load(j):
        return pltpu.make_async_copy(
            w_ref.at[:, pl.ds(pl.multiple_of(j * chunk, chunk), chunk)],
            w_all.at[j, z, c], w_load.at[j],
        )

    def w_copy(j, plane, way):
        device = (at(z - 1, y, c, x), at(z + 1, y, c, x), sibling)[way]
        block = w_all.at[j, plane, c]
        return remote(block, block, w_send.at[j, plane, way], w_recv.at[j, plane, c], device)

    def w_arrive(j, plane, core):
        block = w_all.at[j, plane, core]
        remote(block, block, w_send.at[j, plane, 2], w_recv.at[j, plane, core], sibling).wait_recv()

    def each(body, count=planes):
        def step(i, carry):
            body(i)
            return carry
        lax.fori_loop(0, count, step, 0)

    every_chunk = functools.partial(each, count=chunks)
    every_chunk(lambda j: load(j).start())
    inputs = [
        pltpu.make_async_copy(src, dst, in_load.at[n])
        for n, (src, dst) in enumerate(
            ((k_in, k_ref), (v_in, v_ref), (q_in, q_ref), (gain_in, gain_ref))
        )
    ]
    for copy in inputs:
        copy.start()

    barrier = pltpu.get_barrier_semaphore()
    for device in (sibling, across, beside, diagonal):
        pl.semaphore_signal(barrier, inc=1, device_id=device, device_id_type=MESH)

    @pl.when(z > 0)
    def _():
        pl.semaphore_signal(barrier, inc=1, device_id=at(z - 1, y, c, x), device_id_type=MESH)

    @pl.when(z < planes - 1)
    def _():
        pl.semaphore_signal(barrier, inc=1, device_id=at(z + 1, y, c, x), device_id_type=MESH)

    pl.semaphore_wait(barrier, 4 + jnp.where(z > 0, 1, 0) + jnp.where(z < planes - 1, 1, 0))

    def send_own(j):
        load(j).wait()

        @pl.when(z > 0)
        def _():
            w_copy(j, z, 0).start()

        @pl.when(z < planes - 1)
        def _():
            w_copy(j, z, 1).start()

    every_chunk(send_own)
    for copy in inputs:
        copy.wait()

    lane = lax.broadcasted_iota(jnp.int32, (1, width), 1)
    in_head = [
        jnp.where((lane >= h * HEAD_DIM) & (lane < (h + 1) * HEAD_DIM), 1.0, 0.0)
        for h in range(group_heads)
    ]
    in_head16 = [m.astype(BF16) for m in in_head]

    def columns(i, yy):
        return pl.ds(pl.multiple_of(i * (2 * width), 2 * width) + yy * width, width)

    def state_copy(i, yy):
        return remote(
            state_own.at[i, yy], state_in.at[i, yy], state_send.at[i, yy], state_recv.at[i, yy], across
        )

    @pl.when(x == 0)
    def _():
        def states(i):
            for yy in range(2):
                full = lax.dot_general(
                    k_ref[:, columns(i, yy)], v_ref[:, columns(i, yy)],
                    (((0,), (0,)), ((), ())), preferred_element_type=F32,
                )
                folded = full[:HEAD_DIM] * in_head[0]
                for h in range(1, group_heads):
                    folded = folded + full[h * HEAD_DIM:(h + 1) * HEAD_DIM] * in_head[h]
                state_own[i, yy] = folded.astype(BF16)
                state_copy(i, yy).start()
        each(states)

    def pass_on(j, distance):
        @pl.when(z - distance >= 0)
        def _():
            w_arrive(j, z - distance, c)

            @pl.when(z < planes - 1)
            def _():
                w_copy(j, z - distance, 1).start()

            if distance > 1:
                w_copy(j, z - distance, 2).start()

        @pl.when(z + distance < planes)
        def _():
            w_arrive(j, z + distance, c)

            @pl.when(z > 0)
            def _():
                w_copy(j, z + distance, 0).start()

            if distance > 1:
                w_copy(j, z + distance, 2).start()

    def x_near(i, yy):
        return remote(
            x_out.at[i, yy], x_all.at[i, y, x], x_send.at[i, yy, 0], x_recv.at[i, y, x], at(z, yy, c, x)
        )

    def x_far(i, yy):
        return remote(
            x_out.at[i, yy], x_all.at[i, y, x], x_send.at[i, yy, 1], x_recv.at[i, y, x],
            at(z, yy, c, 1 - x),
        )

    causal = (
        lax.broadcasted_iota(jnp.int32, (tok, tok), 0) >= lax.broadcasted_iota(jnp.int32, (tok, tok), 1)
    )
    ms[x] = jnp.zeros(ms.shape[1:], F32)

    def pass_on_share(i, distance):
        share = chunks // planes
        each(lambda n: pass_on(i * share + n, distance), share)

    def deliver(i, yy, attn):
        ms[x] += jnp.broadcast_to(
            jnp.sum(attn * attn, axis=-1, keepdims=True) * (1.0 / features), ms.shape[1:]
        )
        scaled = (attn * gain_ref[:, columns(i, yy)]).astype(BF16)
        x_out[i, yy] = scaled
        x_far(i, yy).start()

        @pl.when(y != yy)
        def _():
            x_near(i, yy).start()

        @pl.when(y == yy)
        def _():
            x_all[i, y, x] = scaled

    def attend(i):
        for yy in range(2):
            q, k, v = (ref[:, columns(i, yy)] for ref in (q_ref, k_ref, v_ref))
            total = jnp.zeros((tok, width), F32)
            for h in range(group_heads):
                scores = lax.dot_general(
                    q * in_head16[h], k, (((1,), (1,)), ((), ())), preferred_element_type=F32
                )
                scores = jnp.where(causal, scores, 0.0).astype(BF16)
                total = total + jnp.dot(scores, v * in_head16[h], preferred_element_type=F32)
            att[i, yy] = total

            @pl.when(x == 0)
            def _():
                deliver(i, yy, att[i, yy])

        pass_on_share(i, 1)

    each(attend)

    every_chunk(lambda j: w_copy(j, z, 2).start())

    def share_near(j):
        @pl.when(z > 0)
        def _():
            w_copy(j, z - 1, 2).start()

        @pl.when(z < planes - 1)
        def _():
            w_copy(j, z + 1, 2).start()

    def attend_earlier(i):
        @pl.when(x == 1)
        def _():
            for yy in range(2):
                state_copy(i, yy).wait_recv()
                state = state_in[i, yy]
                wide = jnp.concatenate([state * m for m in in_head16], axis=0)
                inter = jnp.dot(q_ref[:, columns(i, yy)], wide, preferred_element_type=F32)
                deliver(i, yy, att[i, yy] + inter)

        pass_on_share(i, 2)
        each(lambda n: share_near(i * (chunks // planes) + n), chunks // planes)

    each(attend_earlier)
    ms_copy = remote(ms.at[x], ms.at[x], ms_send, ms_recv, across)
    ms_copy.start()

    def x_arrive(i, yy, xx):
        remote(
            x_all.at[i, yy, xx], x_all.at[i, yy, xx], x_send.at[i, yy, 1], x_recv.at[i, yy, xx], across
        ).wait_recv()

    def merge(i):
        x_arrive(i, y, 1 - x)
        x_arrive(i, 1 - y, x)
        x_arrive(i, 1 - y, 1 - x)
        parts = [x_all[i, yy, xx].astype(F32) for yy in range(2) for xx in range(2)]
        x_cat[i] = jnp.concatenate(parts, axis=0).astype(BF16)

    each(merge)

    def multiply(j, plane):
        w_arrive(j, plane, 1 - c)
        return jnp.dot(
            x_cat[plane], w_all[j, plane].reshape(width, chunk), preferred_element_type=F32
        )

    def first(j):
        total = multiply(j, z)
        acc[j, 0] = total[:2 * tok]
        acc[j, 1] = total[2 * tok:]

    every_chunk(first)

    def add(j, plane):
        total = multiply(j, plane)
        acc[j, 0] += total[:2 * tok]
        acc[j, 1] += total[2 * tok:]

    def add_both(j, distance):
        @pl.when(z - distance >= 0)
        def _():
            add(j, z - distance)

        @pl.when(z + distance < planes)
        def _():
            add(j, z + distance)

    for distance in range(1, planes - 1):
        every_chunk(functools.partial(add_both, distance=distance))

    def part_copy(j):
        return remote(part_out.at[j], part_in.at[j], part_send.at[j], part_recv.at[j], beside)

    def last(j):
        pass_on(j, planes - 1)
        add_both(j, planes - 1)
        part_out[j] = acc[j, 1 - y].astype(BF16)
        part_copy(j).start()

    every_chunk(last)

    remote(ms.at[1 - x], ms.at[1 - x], ms_send, ms_recv, across).wait_recv()
    mean_sq = jnp.concatenate([ms[0][:, :1], ms[1][:, :1]], axis=0)
    scale = lax.rsqrt(mean_sq + 1e-05)

    def finish(j):
        part_copy(j).wait_recv()
        total = acc[j, y] + part_in[j].astype(F32)
        out_ref[:, pl.ds(pl.multiple_of(j * chunk, chunk), chunk)] = (total * scale).astype(BF16)

    every_chunk(finish)

    def drain(i):
        for yy in range(2):
            x_far(i, yy).wait_send()

            @pl.when(y != yy)
            def _():
                x_near(i, yy).wait_send()

            @pl.when(x == 0)
            def _():
                state_copy(i, yy).wait_send()

    def drain_chunk(i):
        part_copy(i).wait_send()

        for plane in range(planes):
            w_copy(i, plane, 2).wait_send()

            @pl.when((plane >= z) & (z > 0))
            def _():
                w_copy(i, plane, 0).wait_send()

            @pl.when((plane <= z) & (z < planes - 1))
            def _():
                w_copy(i, plane, 1).wait_send()

    each(drain)
    every_chunk(drain_chunk)
    ms_copy.wait_send()


def fused(planes, chunks, queries, keys, values, norm_gain, out_weight):
    tok, features = queries.shape
    rows, out_columns = out_weight.shape
    width, chunk = 2 * rows, out_columns // chunks
    hbm = pl.BlockSpec(memory_space=pltpu.HBM)
    dma = pltpu.SemaphoreType.DMA
    return pl.pallas_call(
        functools.partial(kernel, planes, chunks),
        out_shape=jax.ShapeDtypeStruct((2 * tok, out_columns), BF16),
        in_specs=[hbm] * 5,
        out_specs=pl.BlockSpec(memory_space=pltpu.VMEM),
        scratch_shapes=[
            pltpu.VMEM((tok, features), BF16),
            pltpu.VMEM((tok, features), BF16),
            pltpu.VMEM((tok, features), BF16),
            pltpu.VMEM((1, features), F32),
            pltpu.VMEM((chunks, planes, 2, rows, chunk), BF16),
            pltpu.VMEM((planes, 2, HEAD_DIM, width), BF16),
            pltpu.VMEM((planes, 2, HEAD_DIM, width), BF16),
            pltpu.VMEM((planes, 2, tok, width), BF16),
            pltpu.VMEM((planes, 2, 2, tok, width), BF16),
            pltpu.VMEM((planes, 4 * tok, width), BF16),
            pltpu.VMEM((planes, 2, tok, width), F32),
            pltpu.VMEM((2, tok, 128), F32),
            pltpu.VMEM((chunks, 2, 2 * tok, chunk), F32),
            pltpu.VMEM((chunks, 2 * tok, chunk), BF16),
            pltpu.VMEM((chunks, 2 * tok, chunk), BF16),
            dma((chunks,)),
            dma((chunks, planes, 3)),
            dma((chunks, planes, 2)),
            dma((planes, 2)),
            dma((planes, 2)),
            dma((planes, 2, 2)),
            dma((planes, 2, 2)),
            dma,
            dma,
            dma((chunks,)),
            dma((chunks,)),
            dma((4,)),
        ],
        compiler_params=pltpu.CompilerParams(
            collective_id=0, has_side_effects=True, vmem_limit_bytes=40 * 1024 * 1024
        ),
    )(queries, keys, values, norm_gain.reshape(1, features), out_weight)


def solution(mesh):
    placed = (
        P(("fsdp", "ctx"), None),
        P(("fsdp", "ctx"), None),
        P(("fsdp", "ctx"), None),
        P(),
        P("fsdp", "ctx"),
    )
    planes = mesh.shape["fsdp"] // 4
    chunks = planes

    def body(queries, keys, values, norm_gain, out_weight):
        rows, out_columns = out_weight.shape
        width = 2 * rows
        fits = (
            mesh.shape["ctx"] == 2
            and mesh.shape["fsdp"] == 4 * planes
            and planes == 4
            and rows % 16 == 0
            and width % HEAD_DIM == 0
            and width % 128 == 0
            and out_columns % (128 * chunks) == 0
        )
        if fits:
            return fused(planes, chunks, queries, keys, values, norm_gain, out_weight)
        return on_device(queries, keys, values, norm_gain, out_weight)

    return jax.shard_map(
        body, mesh=mesh, in_specs=placed, out_specs=P("fsdp", "ctx"), check_vma=False
    )
```

```python
import functools

import jax
import jax.numpy as jnp
from jax import lax
from jax.experimental import pallas as pl
from jax.experimental.pallas import tpu as pltpu
from jax.sharding import PartitionSpec as P

HEADS = 32
HEAD_DIM = 96
MESH = pl.DeviceIdType.MESH
BF16 = jnp.bfloat16
F32 = jnp.float32


def on_device(queries, keys, values, norm_gain, out_weight):
    tok_rows = queries.shape[0]
    q_heads = queries.reshape(tok_rows, HEADS, HEAD_DIM)
    k_heads = keys.reshape(tok_rows, HEADS, HEAD_DIM)
    v_heads = values.reshape(tok_rows, HEADS, HEAD_DIM)
    scores = jnp.einsum("thd,shd->hts", q_heads, k_heads, preferred_element_type=jnp.float32)
    causal = jnp.arange(tok_rows)[:, None] >= jnp.arange(tok_rows)[None, :]
    scores = jnp.where(causal, scores, 0.0).astype(jnp.bfloat16)
    intra = jnp.einsum("hts,shd->thd", scores, v_heads, preferred_element_type=jnp.float32)
    local_state = jnp.einsum("shd,she->hde", k_heads, v_heads, preferred_element_type=jnp.float32)
    flat_state = local_state.reshape(HEADS, HEAD_DIM * HEAD_DIM).astype(jnp.bfloat16)
    every_state = lax.all_gather(flat_state[None], "ctx", axis=0, tiled=True)
    position = lax.axis_index("ctx")
    earlier = (jnp.arange(every_state.shape[0]) < position)[:, None, None]
    prefix_flat = jnp.sum(jnp.where(earlier, every_state.astype(jnp.float32), 0.0), axis=0)
    prefix_state = prefix_flat.reshape(HEADS, HEAD_DIM, HEAD_DIM).astype(jnp.bfloat16)
    inter = jnp.einsum("thd,hde->the", q_heads, prefix_state, preferred_element_type=jnp.float32)
    attn = (intra + inter).reshape(tok_rows, HEADS * HEAD_DIM)
    mean_sq = jnp.mean(attn * attn, axis=-1, keepdims=True)
    normed = (attn * lax.rsqrt(mean_sq + 1e-05) * norm_gain).astype(jnp.bfloat16)
    weight_block = lax.all_gather(out_weight, "fsdp", axis=0, tiled=True)
    result = jnp.dot(
        lax.all_gather(normed, "ctx", axis=0, tiled=True),
        weight_block,
        preferred_element_type=jnp.float32,
    )
    return result.astype(jnp.bfloat16)


def kernel(
    planes, chunks, q_in, k_in, v_in, gain_in, w_ref, out_ref,
    q_ref, k_ref, v_ref, gain_ref, w_all, out_all, state_own, state_in, x_out, x_all, x_cat, att, ms, acc, part_out, part_in,
    w_load, w_send, w_recv, state_send, state_recv, x_send, x_recv, ms_send, ms_recv,
    part_send, part_recv, in_load, out_store,
):
    tok, features = q_ref.shape
    rows = w_ref.shape[0]
    width = 2 * rows
    chunk = w_ref.shape[1] // chunks
    group_heads = width // HEAD_DIM

    f = lax.axis_index("fsdp")
    x = lax.axis_index("ctx")
    z, y, c = lax.div(f, 4), lax.rem(lax.div(f, 2), 2), lax.rem(f, 2)

    def at(zz, yy, cc, xx):
        return (4 * zz + 2 * yy + cc, xx)

    sibling = at(z, y, 1 - c, x)
    across = at(z, y, c, 1 - x)
    beside = at(z, 1 - y, c, x)
    diagonal = at(z, 1 - y, c, 1 - x)

    def remote(src, dst, send, recv, device):
        return pltpu.make_async_remote_copy(
            src_ref=src, dst_ref=dst, send_sem=send, recv_sem=recv,
            device_id=device, device_id_type=MESH,
        )

    def load(j):
        return pltpu.make_async_copy(
            w_ref.at[:, pl.ds(pl.multiple_of(j * chunk, chunk), chunk)],
            w_all.at[j, z, c], w_load.at[j],
        )

    def w_copy(j, plane, way):
        device = (at(z - 1, y, c, x), at(z + 1, y, c, x), sibling)[way]
        block = w_all.at[j, plane, c]
        return remote(block, block, w_send.at[j, plane, way], w_recv.at[j, plane, c], device)

    def w_arrive(j, plane, core):
        block = w_all.at[j, plane, core]
        remote(block, block, w_send.at[j, plane, 2], w_recv.at[j, plane, core], sibling).wait_recv()

    def each(body, count=planes):
        def step(i, carry):
            body(i)
            return carry
        lax.fori_loop(0, count, step, 0)

    every_chunk = functools.partial(each, count=chunks)
    every_chunk(lambda j: load(j).start())
    inputs = [
        pltpu.make_async_copy(src, dst, in_load.at[n])
        for n, (src, dst) in enumerate(
            ((k_in, k_ref), (v_in, v_ref), (q_in, q_ref), (gain_in, gain_ref))
        )
    ]
    for copy in inputs:
        copy.start()

    barrier = pltpu.get_barrier_semaphore()
    for device in (sibling, across, beside, diagonal):
        pl.semaphore_signal(barrier, inc=1, device_id=device, device_id_type=MESH)

    @pl.when(z > 0)
    def _():
        pl.semaphore_signal(barrier, inc=1, device_id=at(z - 1, y, c, x), device_id_type=MESH)

    @pl.when(z < planes - 1)
    def _():
        pl.semaphore_signal(barrier, inc=1, device_id=at(z + 1, y, c, x), device_id_type=MESH)

    pl.semaphore_wait(barrier, 4 + jnp.where(z > 0, 1, 0) + jnp.where(z < planes - 1, 1, 0))

    def send_own(j):
        load(j).wait()

        @pl.when(z > 0)
        def _():
            w_copy(j, z, 0).start()

        @pl.when(z < planes - 1)
        def _():
            w_copy(j, z, 1).start()

        w_copy(j, z, 2).start()

    every_chunk(send_own)
    for copy in inputs:
        copy.wait()

    lane = lax.broadcasted_iota(jnp.int32, (1, width), 1)
    in_head = [
        jnp.where((lane >= h * HEAD_DIM) & (lane < (h + 1) * HEAD_DIM), 1.0, 0.0)
        for h in range(group_heads)
    ]
    in_head16 = [m.astype(BF16) for m in in_head]

    def columns(i, yy):
        return pl.ds(pl.multiple_of(i * (2 * width), 2 * width) + yy * width, width)

    def state_copy(i, yy):
        return remote(
            state_own.at[i, yy], state_in.at[i, yy], state_send.at[i, yy], state_recv.at[i, yy], across
        )

    @pl.when(x == 0)
    def _():
        def states(i):
            for yy in range(2):
                full = lax.dot_general(
                    k_ref[:, columns(i, yy)], v_ref[:, columns(i, yy)],
                    (((0,), (0,)), ((), ())), preferred_element_type=F32,
                )
                folded = full[:HEAD_DIM] * in_head[0]
                for h in range(1, group_heads):
                    folded = folded + full[h * HEAD_DIM:(h + 1) * HEAD_DIM] * in_head[h]
                state_own[i, yy] = folded.astype(BF16)
                state_copy(i, yy).start()
        each(states)

    def pass_on(j, distance):
        @pl.when(z - distance >= 0)
        def _():
            w_arrive(j, z - distance, c)

            @pl.when(z < planes - 1)
            def _():
                w_copy(j, z - distance, 1).start()

            w_copy(j, z - distance, 2).start()

        @pl.when(z + distance < planes)
        def _():
            w_arrive(j, z + distance, c)

            @pl.when(z > 0)
            def _():
                w_copy(j, z + distance, 0).start()

            w_copy(j, z + distance, 2).start()

    def x_near(i, yy):
        return remote(
            x_out.at[i, yy], x_all.at[i, y, x], x_send.at[i, yy, 0], x_recv.at[i, y, x], at(z, yy, c, x)
        )

    def x_far(i, yy):
        return remote(
            x_out.at[i, yy], x_all.at[i, y, x], x_send.at[i, yy, 1], x_recv.at[i, y, x],
            at(z, yy, c, 1 - x),
        )

    causal = (
        lax.broadcasted_iota(jnp.int32, (tok, tok), 0) >= lax.broadcasted_iota(jnp.int32, (tok, tok), 1)
    )
    ms[x] = jnp.zeros(ms.shape[1:], F32)

    def pass_on_share(i, distance):
        share = chunks // planes
        each(lambda n: pass_on(i * share + n, distance), share)

    def deliver(i, yy, attn):
        ms[x] += jnp.broadcast_to(
            jnp.sum(attn * attn, axis=-1, keepdims=True) * (1.0 / features), ms.shape[1:]
        )
        scaled = (attn * gain_ref[:, columns(i, yy)]).astype(BF16)
        x_out[i, yy] = scaled
        x_far(i, yy).start()

        @pl.when(y != yy)
        def _():
            x_near(i, yy).start()

        @pl.when(y == yy)
        def _():
            x_all[i, y, x] = scaled

    def attend(i):
        for yy in range(2):
            q, k, v = (ref[:, columns(i, yy)] for ref in (q_ref, k_ref, v_ref))
            total = jnp.zeros((tok, width), F32)
            for h in range(group_heads):
                scores = lax.dot_general(
                    q * in_head16[h], k, (((1,), (1,)), ((), ())), preferred_element_type=F32
                )
                scores = jnp.where(causal, scores, 0.0).astype(BF16)
                total = total + jnp.dot(scores, v * in_head16[h], preferred_element_type=F32)
            att[i, yy] = total

            @pl.when(x == 1)
            def _():
                state_copy(i, yy).wait_recv()
                state = state_in[i, yy]
                wide = jnp.concatenate([state * m for m in in_head16], axis=0)
                att[i, yy] += jnp.dot(q, wide, preferred_element_type=F32)

            deliver(i, yy, att[i, yy])

        pass_on_share(i, 1)

    each(attend)
    every_chunk(lambda j: pass_on(j, 2))

    ms_copy = remote(ms.at[x], ms.at[x], ms_send, ms_recv, across)
    ms_copy.start()

    def x_arrive(i, yy, xx):
        remote(
            x_all.at[i, yy, xx], x_all.at[i, yy, xx], x_send.at[i, yy, 1], x_recv.at[i, yy, xx], across
        ).wait_recv()

    def merge(i):
        x_arrive(i, y, 1 - x)
        x_arrive(i, 1 - y, x)
        x_arrive(i, 1 - y, 1 - x)
        parts = [x_all[i, yy, xx].astype(F32) for yy in range(2) for xx in range(2)]
        x_cat[i] = jnp.concatenate(parts, axis=0).astype(BF16)

    each(merge)

    def multiply(j, plane):
        w_arrive(j, plane, 1 - c)
        return jnp.dot(
            x_cat[plane], w_all[j, plane].reshape(width, chunk), preferred_element_type=F32
        )

    def first(j):
        total = multiply(j, z)
        acc[j, 0] = total[:2 * tok]
        acc[j, 1] = total[2 * tok:]

    every_chunk(first)

    def add(j, plane):
        total = multiply(j, plane)
        acc[j, 0] += total[:2 * tok]
        acc[j, 1] += total[2 * tok:]

    def add_both(j, distance):
        @pl.when(z - distance >= 0)
        def _():
            add(j, z - distance)

        @pl.when(z + distance < planes)
        def _():
            add(j, z + distance)

    for distance in range(1, planes - 1):
        every_chunk(functools.partial(add_both, distance=distance))

    def part_copy(j):
        return remote(part_out.at[j], part_in.at[j], part_send.at[j], part_recv.at[j], beside)

    def last(j):
        pass_on(j, planes - 1)
        add_both(j, planes - 1)
        part_out[j] = acc[j, 1 - y].astype(BF16)
        part_copy(j).start()

    every_chunk(last)

    remote(ms.at[1 - x], ms.at[1 - x], ms_send, ms_recv, across).wait_recv()
    mean_sq = jnp.concatenate([ms[0][:, :1], ms[1][:, :1]], axis=0)
    scale = lax.rsqrt(mean_sq + 1e-05)

    def store(j):
        return pltpu.make_async_copy(
            out_all.at[j],
            out_ref.at[:, pl.ds(pl.multiple_of(j * chunk, chunk), chunk)], out_store.at[j],
        )

    def finish(j):
        part_copy(j).wait_recv()
        total = acc[j, y] + part_in[j].astype(F32)
        out_all[j] = (total * scale).astype(BF16)
        store(j).start()

    every_chunk(finish)

    def drain(i):
        for yy in range(2):
            x_far(i, yy).wait_send()

            @pl.when(y != yy)
            def _():
                x_near(i, yy).wait_send()

            @pl.when(x == 0)
            def _():
                state_copy(i, yy).wait_send()

    def drain_chunk(i):
        part_copy(i).wait_send()
        store(i).wait()

        for plane in range(planes):
            w_copy(i, plane, 2).wait_send()

            @pl.when((plane >= z) & (z > 0))
            def _():
                w_copy(i, plane, 0).wait_send()

            @pl.when((plane <= z) & (z < planes - 1))
            def _():
                w_copy(i, plane, 1).wait_send()

    each(drain)
    every_chunk(drain_chunk)
    ms_copy.wait_send()


def fused(planes, chunks, queries, keys, values, norm_gain, out_weight):
    tok, features = queries.shape
    rows, out_columns = out_weight.shape
    width, chunk = 2 * rows, out_columns // chunks
    anywhere = pl.BlockSpec(memory_space=pl.ANY)
    dma = pltpu.SemaphoreType.DMA
    return pl.pallas_call(
        functools.partial(kernel, planes, chunks),
        out_shape=jax.ShapeDtypeStruct((2 * tok, out_columns), BF16),
        in_specs=[anywhere] * 5,
        out_specs=anywhere,
        scratch_shapes=[
            pltpu.VMEM((tok, features), BF16),
            pltpu.VMEM((tok, features), BF16),
            pltpu.VMEM((tok, features), BF16),
            pltpu.VMEM((1, features), F32),
            pltpu.VMEM((chunks, planes, 2, rows, chunk), BF16),
            pltpu.VMEM((chunks, 2 * tok, chunk), BF16),
            pltpu.VMEM((planes, 2, HEAD_DIM, width), BF16),
            pltpu.VMEM((planes, 2, HEAD_DIM, width), BF16),
            pltpu.VMEM((planes, 2, tok, width), BF16),
            pltpu.VMEM((planes, 2, 2, tok, width), BF16),
            pltpu.VMEM((planes, 4 * tok, width), BF16),
            pltpu.VMEM((planes, 2, tok, width), F32),
            pltpu.VMEM((2, tok, 128), F32),
            pltpu.VMEM((chunks, 2, 2 * tok, chunk), F32),
            pltpu.VMEM((chunks, 2 * tok, chunk), BF16),
            pltpu.VMEM((chunks, 2 * tok, chunk), BF16),
            dma((chunks,)),
            dma((chunks, planes, 3)),
            dma((chunks, planes, 2)),
            dma((planes, 2)),
            dma((planes, 2)),
            dma((planes, 2, 2)),
            dma((planes, 2, 2)),
            dma,
            dma,
            dma((chunks,)),
            dma((chunks,)),
            dma((4,)),
            dma((chunks,)),
        ],
        compiler_params=pltpu.CompilerParams(
            collective_id=0, has_side_effects=True, vmem_limit_bytes=56 * 1024 * 1024
        ),
    )(queries, keys, values, norm_gain.reshape(1, features), out_weight)


def solution(mesh):
    placed = (
        P(("fsdp", "ctx"), None),
        P(("fsdp", "ctx"), None),
        P(("fsdp", "ctx"), None),
        P(),
        P("fsdp", "ctx"),
    )
    planes = mesh.shape["fsdp"] // 4
    chunks = planes

    def body(queries, keys, values, norm_gain, out_weight):
        rows, out_columns = out_weight.shape
        width = 2 * rows
        fits = (
            mesh.shape["ctx"] == 2
            and mesh.shape["fsdp"] == 4 * planes
            and planes == 4
            and rows % 16 == 0
            and width % HEAD_DIM == 0
            and width % 128 == 0
            and out_columns % (128 * chunks) == 0
        )
        if fits:
            return fused(planes, chunks, queries, keys, values, norm_gain, out_weight)
        return on_device(queries, keys, values, norm_gain, out_weight)

    return jax.shard_map(
        body, mesh=mesh, in_specs=placed, out_specs=P("fsdp", "ctx"), check_vma=False
    )
```

```python
import functools

import jax
import jax.numpy as jnp
from jax import lax
from jax.experimental import pallas as pl
from jax.experimental.pallas import tpu as pltpu
from jax.sharding import PartitionSpec as P

HEADS = 32
HEAD_DIM = 96
MESH = pl.DeviceIdType.MESH
BF16 = jnp.bfloat16
F32 = jnp.float32


def on_device(queries, keys, values, norm_gain, out_weight):
    tok_rows = queries.shape[0]
    q_heads = queries.reshape(tok_rows, HEADS, HEAD_DIM)
    k_heads = keys.reshape(tok_rows, HEADS, HEAD_DIM)
    v_heads = values.reshape(tok_rows, HEADS, HEAD_DIM)
    scores = jnp.einsum("thd,shd->hts", q_heads, k_heads, preferred_element_type=jnp.float32)
    causal = jnp.arange(tok_rows)[:, None] >= jnp.arange(tok_rows)[None, :]
    scores = jnp.where(causal, scores, 0.0).astype(jnp.bfloat16)
    intra = jnp.einsum("hts,shd->thd", scores, v_heads, preferred_element_type=jnp.float32)
    local_state = jnp.einsum("shd,she->hde", k_heads, v_heads, preferred_element_type=jnp.float32)
    flat_state = local_state.reshape(HEADS, HEAD_DIM * HEAD_DIM).astype(jnp.bfloat16)
    every_state = lax.all_gather(flat_state[None], "ctx", axis=0, tiled=True)
    position = lax.axis_index("ctx")
    earlier = (jnp.arange(every_state.shape[0]) < position)[:, None, None]
    prefix_flat = jnp.sum(jnp.where(earlier, every_state.astype(jnp.float32), 0.0), axis=0)
    prefix_state = prefix_flat.reshape(HEADS, HEAD_DIM, HEAD_DIM).astype(jnp.bfloat16)
    inter = jnp.einsum("thd,hde->the", q_heads, prefix_state, preferred_element_type=jnp.float32)
    attn = (intra + inter).reshape(tok_rows, HEADS * HEAD_DIM)
    mean_sq = jnp.mean(attn * attn, axis=-1, keepdims=True)
    normed = (attn * lax.rsqrt(mean_sq + 1e-05) * norm_gain).astype(jnp.bfloat16)
    weight_block = lax.all_gather(out_weight, "fsdp", axis=0, tiled=True)
    result = jnp.dot(
        lax.all_gather(normed, "ctx", axis=0, tiled=True),
        weight_block,
        preferred_element_type=jnp.float32,
    )
    return result.astype(jnp.bfloat16)


def kernel(
    planes, chunks, q_in, k_in, v_in, gain_in, w_ref, out_ref,
    q_ref, k_ref, v_ref, gain_ref, w_all, out_all, state_own, state_in, x_out, x_all, x_cat, att, ms, acc, part_out, part_in,
    w_load, w_send, w_recv, state_send, state_recv, x_send, x_recv, ms_send, ms_recv,
    part_send, part_recv, in_load, out_store,
):
    tok, features = q_ref.shape
    rows = w_ref.shape[0]
    width = 2 * rows
    chunk = w_ref.shape[1] // chunks
    group_heads = width // HEAD_DIM

    f = lax.axis_index("fsdp")
    x = lax.axis_index("ctx")
    z, y, c = lax.div(f, 4), lax.rem(lax.div(f, 2), 2), lax.rem(f, 2)

    def at(zz, yy, cc, xx):
        return (4 * zz + 2 * yy + cc, xx)

    sibling = at(z, y, 1 - c, x)
    across = at(z, y, c, 1 - x)
    beside = at(z, 1 - y, c, x)
    diagonal = at(z, 1 - y, c, 1 - x)

    def remote(src, dst, send, recv, device):
        return pltpu.make_async_remote_copy(
            src_ref=src, dst_ref=dst, send_sem=send, recv_sem=recv,
            device_id=device, device_id_type=MESH,
        )

    def load(j):
        return pltpu.make_async_copy(
            w_ref.at[:, pl.ds(pl.multiple_of(j * chunk, chunk), chunk)],
            w_all.at[j, z, c], w_load.at[j],
        )

    def w_copy(j, plane, way):
        device = (at(z - 1, y, c, x), at(z + 1, y, c, x), sibling)[way]
        block = w_all.at[j, plane, c]
        return remote(block, block, w_send.at[j, plane, way], w_recv.at[j, plane, c], device)

    def w_arrive(j, plane, core):
        block = w_all.at[j, plane, core]
        remote(block, block, w_send.at[j, plane, 2], w_recv.at[j, plane, core], sibling).wait_recv()

    def each(body, count=planes):
        def step(i, carry):
            body(i)
            return carry
        lax.fori_loop(0, count, step, 0)

    every_chunk = functools.partial(each, count=chunks)
    every_chunk(lambda j: load(j).start())
    inputs = [
        pltpu.make_async_copy(src, dst, in_load.at[n])
        for n, (src, dst) in enumerate(
            ((k_in, k_ref), (v_in, v_ref), (q_in, q_ref), (gain_in, gain_ref))
        )
    ]
    for copy in inputs:
        copy.start()

    barrier = pltpu.get_barrier_semaphore()
    for device in (sibling, across, beside, diagonal):
        pl.semaphore_signal(barrier, inc=1, device_id=device, device_id_type=MESH)

    @pl.when(z > 0)
    def _():
        pl.semaphore_signal(barrier, inc=1, device_id=at(z - 1, y, c, x), device_id_type=MESH)

    @pl.when(z < planes - 1)
    def _():
        pl.semaphore_signal(barrier, inc=1, device_id=at(z + 1, y, c, x), device_id_type=MESH)

    pl.semaphore_wait(barrier, 4 + jnp.where(z > 0, 1, 0) + jnp.where(z < planes - 1, 1, 0))

    def send_own(j):
        load(j).wait()

        @pl.when(z > 0)
        def _():
            w_copy(j, z, 0).start()

        @pl.when(z < planes - 1)
        def _():
            w_copy(j, z, 1).start()

        w_copy(j, z, 2).start()

    every_chunk(send_own)
    for copy in inputs:
        copy.wait()

    lane = lax.broadcasted_iota(jnp.int32, (1, width), 1)
    in_head = [
        jnp.where((lane >= h * HEAD_DIM) & (lane < (h + 1) * HEAD_DIM), 1.0, 0.0)
        for h in range(group_heads)
    ]
    in_head16 = [m.astype(BF16) for m in in_head]

    def columns(i, yy):
        return pl.ds(pl.multiple_of(i * (2 * width), 2 * width) + yy * width, width)

    def state_copy(i, yy):
        return remote(
            state_own.at[i, yy], state_in.at[i, yy], state_send.at[i, yy], state_recv.at[i, yy], across
        )

    @pl.when(x == 0)
    def _():
        def states(i):
            for yy in range(2):
                full = lax.dot_general(
                    k_ref[:, columns(i, yy)], v_ref[:, columns(i, yy)],
                    (((0,), (0,)), ((), ())), preferred_element_type=F32,
                )
                folded = full[:HEAD_DIM] * in_head[0]
                for h in range(1, group_heads):
                    folded = folded + full[h * HEAD_DIM:(h + 1) * HEAD_DIM] * in_head[h]
                state_own[i, yy] = folded.astype(BF16)
                state_copy(i, yy).start()
        each(states)

    def pass_on(j, distance):
        @pl.when(z - distance >= 0)
        def _():
            w_arrive(j, z - distance, c)

            @pl.when(z < planes - 1)
            def _():
                w_copy(j, z - distance, 1).start()

            w_copy(j, z - distance, 2).start()

        @pl.when(z + distance < planes)
        def _():
            w_arrive(j, z + distance, c)

            @pl.when(z > 0)
            def _():
                w_copy(j, z + distance, 0).start()

            w_copy(j, z + distance, 2).start()

    def x_near(i, yy):
        return remote(
            x_out.at[i, yy], x_all.at[i, y, x], x_send.at[i, yy, 0], x_recv.at[i, y, x], at(z, yy, c, x)
        )

    def x_far(i, yy):
        return remote(
            x_out.at[i, yy], x_all.at[i, y, x], x_send.at[i, yy, 1], x_recv.at[i, y, x],
            at(z, yy, c, 1 - x),
        )

    causal = (
        lax.broadcasted_iota(jnp.int32, (tok, tok), 0) >= lax.broadcasted_iota(jnp.int32, (tok, tok), 1)
    )
    ms[x] = jnp.zeros(ms.shape[1:], F32)

    def pass_on_share(i, distance):
        share = chunks // planes
        each(lambda n: pass_on(i * share + n, distance), share)

    def deliver(i, yy, attn):
        ms[x] += jnp.broadcast_to(
            jnp.sum(attn * attn, axis=-1, keepdims=True) * (1.0 / features), ms.shape[1:]
        )
        scaled = (attn * gain_ref[:, columns(i, yy)]).astype(BF16)
        x_out[i, yy] = scaled
        x_far(i, yy).start()

        @pl.when(y != yy)
        def _():
            x_near(i, yy).start()

        @pl.when(y == yy)
        def _():
            x_all[i, y, x] = scaled

    def attend(i):
        for yy in range(2):
            q, k, v = (ref[:, columns(i, yy)] for ref in (q_ref, k_ref, v_ref))
            total = jnp.zeros((tok, width), F32)
            for h in range(group_heads):
                scores = lax.dot_general(
                    q * in_head16[h], k, (((1,), (1,)), ((), ())), preferred_element_type=F32
                )
                scores = jnp.where(causal, scores, 0.0).astype(BF16)
                total = total + jnp.dot(scores, v * in_head16[h], preferred_element_type=F32)
            att[i, yy] = total

            @pl.when(x == 1)
            def _():
                state_copy(i, yy).wait_recv()
                state = state_in[i, yy]
                wide = jnp.concatenate([state * m for m in in_head16], axis=0)
                att[i, yy] += jnp.dot(q, wide, preferred_element_type=F32)

            deliver(i, yy, att[i, yy])

        pass_on_share(i, 1)

    each(attend)
    for j in range(planes * (chunks // planes), chunks):
        pass_on(j, 1)
    every_chunk(lambda j: pass_on(j, 2))

    ms_copy = remote(ms.at[x], ms.at[x], ms_send, ms_recv, across)
    ms_copy.start()

    def x_arrive(i, yy, xx):
        remote(
            x_all.at[i, yy, xx], x_all.at[i, yy, xx], x_send.at[i, yy, 1], x_recv.at[i, yy, xx], across
        ).wait_recv()

    def merge(i):
        x_arrive(i, y, 1 - x)
        x_arrive(i, 1 - y, x)
        x_arrive(i, 1 - y, 1 - x)
        parts = [x_all[i, yy, xx].astype(F32) for yy in range(2) for xx in range(2)]
        x_cat[i] = jnp.concatenate(parts, axis=0).astype(BF16)

    each(merge)

    def multiply(j, plane):
        w_arrive(j, plane, 1 - c)
        return jnp.dot(
            x_cat[plane], w_all[j, plane].reshape(width, chunk), preferred_element_type=F32
        )

    def first(j):
        total = multiply(j, z)
        acc[j, 0] = total[:2 * tok]
        acc[j, 1] = total[2 * tok:]

    every_chunk(first)

    def add(j, plane):
        total = multiply(j, plane)
        acc[j, 0] += total[:2 * tok]
        acc[j, 1] += total[2 * tok:]

    def add_both(j, distance):
        @pl.when(z - distance >= 0)
        def _():
            add(j, z - distance)

        @pl.when(z + distance < planes)
        def _():
            add(j, z + distance)

    for distance in range(1, planes - 1):
        every_chunk(functools.partial(add_both, distance=distance))

    def part_copy(j):
        return remote(part_out.at[j], part_in.at[j], part_send.at[j], part_recv.at[j], beside)

    def last(j):
        pass_on(j, planes - 1)
        add_both(j, planes - 1)
        part_out[j] = acc[j, 1 - y].astype(BF16)
        part_copy(j).start()

    every_chunk(last)

    remote(ms.at[1 - x], ms.at[1 - x], ms_send, ms_recv, across).wait_recv()
    mean_sq = jnp.concatenate([ms[0][:, :1], ms[1][:, :1]], axis=0)
    scale = lax.rsqrt(mean_sq + 1e-05)

    def store(j):
        return pltpu.make_async_copy(
            out_all.at[j],
            out_ref.at[:, pl.ds(pl.multiple_of(j * chunk, chunk), chunk)], out_store.at[j],
        )

    def finish(j):
        part_copy(j).wait_recv()
        total = acc[j, y] + part_in[j].astype(F32)
        out_all[j] = (total * scale).astype(BF16)
        store(j).start()

    every_chunk(finish)

    def drain(i):
        for yy in range(2):
            x_far(i, yy).wait_send()

            @pl.when(y != yy)
            def _():
                x_near(i, yy).wait_send()

            @pl.when(x == 0)
            def _():
                state_copy(i, yy).wait_send()

    def drain_chunk(i):
        part_copy(i).wait_send()
        store(i).wait()

        for plane in range(planes):
            w_copy(i, plane, 2).wait_send()

            @pl.when((plane >= z) & (z > 0))
            def _():
                w_copy(i, plane, 0).wait_send()

            @pl.when((plane <= z) & (z < planes - 1))
            def _():
                w_copy(i, plane, 1).wait_send()

    each(drain)
    every_chunk(drain_chunk)
    ms_copy.wait_send()


def fused(planes, chunks, queries, keys, values, norm_gain, out_weight):
    tok, features = queries.shape
    rows, out_columns = out_weight.shape
    width, chunk = 2 * rows, out_columns // chunks
    anywhere = pl.BlockSpec(memory_space=pl.ANY)
    dma = pltpu.SemaphoreType.DMA
    return pl.pallas_call(
        functools.partial(kernel, planes, chunks),
        out_shape=jax.ShapeDtypeStruct((2 * tok, out_columns), BF16),
        in_specs=[anywhere] * 5,
        out_specs=anywhere,
        scratch_shapes=[
            pltpu.VMEM((tok, features), BF16),
            pltpu.VMEM((tok, features), BF16),
            pltpu.VMEM((tok, features), BF16),
            pltpu.VMEM((1, features), F32),
            pltpu.VMEM((chunks, planes, 2, rows, chunk), BF16),
            pltpu.VMEM((chunks, 2 * tok, chunk), BF16),
            pltpu.VMEM((planes, 2, HEAD_DIM, width), BF16),
            pltpu.VMEM((planes, 2, HEAD_DIM, width), BF16),
            pltpu.VMEM((planes, 2, tok, width), BF16),
            pltpu.VMEM((planes, 2, 2, tok, width), BF16),
            pltpu.VMEM((planes, 4 * tok, width), BF16),
            pltpu.VMEM((planes, 2, tok, width), F32),
            pltpu.VMEM((2, tok, 128), F32),
            pltpu.VMEM((chunks, 2, 2 * tok, chunk), F32),
            pltpu.VMEM((chunks, 2 * tok, chunk), BF16),
            pltpu.VMEM((chunks, 2 * tok, chunk), BF16),
            dma((chunks,)),
            dma((chunks, planes, 3)),
            dma((chunks, planes, 2)),
            dma((planes, 2)),
            dma((planes, 2)),
            dma((planes, 2, 2)),
            dma((planes, 2, 2)),
            dma,
            dma,
            dma((chunks,)),
            dma((chunks,)),
            dma((4,)),
            dma((chunks,)),
        ],
        compiler_params=pltpu.CompilerParams(
            collective_id=0, has_side_effects=True, vmem_limit_bytes=56 * 1024 * 1024
        ),
    )(queries, keys, values, norm_gain.reshape(1, features), out_weight)


def solution(mesh):
    placed = (
        P(("fsdp", "ctx"), None),
        P(("fsdp", "ctx"), None),
        P(("fsdp", "ctx"), None),
        P(),
        P("fsdp", "ctx"),
    )
    planes = mesh.shape["fsdp"] // 4
    chunks = 6

    def body(queries, keys, values, norm_gain, out_weight):
        rows, out_columns = out_weight.shape
        width = 2 * rows
        fits = (
            mesh.shape["ctx"] == 2
            and mesh.shape["fsdp"] == 4 * planes
            and planes == 4
            and rows % 16 == 0
            and width % HEAD_DIM == 0
            and width % 128 == 0
            and out_columns % (128 * chunks) == 0
        )
        if fits:
            return fused(planes, chunks, queries, keys, values, norm_gain, out_weight)
        return on_device(queries, keys, values, norm_gain, out_weight)

    return jax.shard_map(
        body, mesh=mesh, in_specs=placed, out_specs=P("fsdp", "ctx"), check_vma=False
    )
```
